32 devices in a mesh: groups: 2 (over y), tensor: 4 (over z), dp: 4 (over x, core).
Axes of the slice: x: 2, y: 2, z: 4, core: 2. Of those that a mesh axis runs over, the one named last changes fastest.
Arguments:
- hidden: bfloat16 [2, 256, 2048], P(None, ('groups', 'dp'), 'tensor'), parts along dimension 1, may hold values from -6 to 6
- attn_gain: bfloat16 [2048], replicated, may hold values from 0.25 to 1.75
- w_qkvz: bfloat16 [2048, 4, 384], P(None, 'tensor'), may hold values from -0.125 to 0.125
- w_ab: bfloat16 [2048, 4, 2], P(None, 'tensor'), may hold values from -0.125 to 0.125
- conv_weight: bfloat16 [4, 4, 256], P(None, 'tensor'), may hold values from -3 to 3
- decay_log: float32 [4], P('tensor'), may hold values from -2 to 1
- dt_bias: float32 [4], P('tensor'), may hold values from -1 to 1
- norm_gain: bfloat16 [128], replicated, may hold values from 0.25 to 1.75
- w_out: bfloat16 [512, 2048], P('tensor'), may hold values from -0.375 to 0.375
- ffn_gain: bfloat16 [2048], replicated, may hold values from 0.25 to 1.75
- w_gu: bfloat16 [2, 2048, 5120], P(None, None, 'tensor'), may hold values from -0.125 to 0.125
- w_down: bfloat16 [5120, 2048], P('tensor'), may hold values from -0.125 to 0.125
- state: float32 [256, 4, 128, 128], P(('groups', 'dp'), 'tensor'), parts along dimension 0, may hold values from -6 to 6
- conv_state: bfloat16 [256, 3, 4, 256], P(('groups', 'dp'), None, 'tensor'), parts along dimension 0, may hold values from -6 to 6
Outputs:
- next_hidden: bfloat16 [2, 256, 2048], P(None, ('groups', 'dp'), 'tensor'), parts along dimension 1
- next_state: float32 [256, 4, 128, 128], P(('groups', 'dp'), 'tensor'), parts along dimension 0
- next_conv: bfloat16 [256, 3, 4, 256], P(('groups', 'dp'), None, 'tensor'), parts along dimension 0
The draws below stay inside these ranges and needn't reach their ends.
There are 2 independent parts, one for each index of `groups`. The reference program is written for one: setup_inputs(seed, part) draws one part's arguments, and reference() takes and returns one part's arrays. A program takes and returns all parts, laid end to end along the dimension named above; an argument that names none is the same for every part. Nothing has to cross between parts.
All inputs are finite; a program needn't handle non-finite values.
Results may differ from the reference program's by a relative error of at most 0.018.
Values may be sent and summed in bfloat16 or wider, within the bound.
A program may use at most 64 MiB of HBM per device.

```python
import jax
import jax.numpy as jnp
from jax import lax

D = 2048
FF = 5120
HEAD = 128
KERNEL = 4
STEPS = 2
SEQS = 128
HV = 4
HK = 2


def raised(entries, own_key, source, target, shards_of, factor):
    owner, partner = [(jnp.arange(entries.shape[dim]) // (entries.shape[dim] // shards_of)).reshape([-1 if axis == dim else 1 for axis in range(entries.ndim)]) for dim in (source, target)]
    chosen = jax.random.permutation(own_key, shards_of)[partner]
    strong = (owner == chosen) | (owner == (partner + shards_of // 2) % shards_of)
    return jnp.where(strong, factor * entries, entries)


def levels(stream_key, extent, cuts, smallest, top_value):
    loudness, own = 1.0, jax.random.fold_in(stream_key, 6)
    for position, shards_of in cuts:
        heights = jnp.exp(jax.random.uniform(jax.random.fold_in(own, position), (shards_of,), jnp.float32, smallest / len(cuts), top_value / len(cuts)))
        loudness = loudness * jnp.repeat(heights, extent[position] // shards_of).reshape([-1 if axis == position else 1 for axis in range(len(extent))])
    return loudness


def scatter_about(own_key, shape, spread, bound, shards=(), held_as=jnp.bfloat16):
    drawn = jax.random.normal(own_key, shape, jnp.float32) * spread
    if len(shards) > 0:
        drawn = levels(own_key, shape, shards, -0.22, 0.18) * drawn
    return jnp.clip(drawn, min=-bound, max=bound).astype(held_as)


def gaussian_with(own_key, extent, deviation, most, cuts, heavy, kind=jnp.bfloat16):
    values = deviation * jax.random.normal(own_key, extent, jnp.float32)
    if cuts:
        values = values * levels(own_key, extent, cuts, -0.22, 0.18)
    return jnp.clip(raised(values, jax.random.fold_in(own_key, 3), *heavy), -most, most).astype(kind)


def setup_inputs(seed: int = 0, part: int = 0) -> dict:
    seeds = jax.random.split(jax.random.key(seed), 15)
    part_splits = jax.random.split(jax.random.fold_in(seeds[14], part), 15)
    return {
        "hidden": scatter_about(part_splits[0], (STEPS, SEQS, D), 1.0, 6.0, ((1, 4), (2, 4))),
        "attn_gain": jnp.clip(1.0 + 0.15 * jax.random.normal(seeds[1], (D,), jnp.float32), 0.25, 1.75).astype(jnp.bfloat16),
        "w_qkvz": scatter_about(seeds[2], (D, HV, 3 * HEAD), D ** -0.5, 0.125, ((1, 4),)),
        "w_ab": scatter_about(seeds[3], (D, HV, 2), D ** -0.5, 0.125, ((1, 4),)),
        "conv_weight": scatter_about(seeds[4], (KERNEL, HV, 2 * HEAD), 0.5, 3.0, ((1, 4),)),
        "decay_log": jnp.clip(-2.0 + 3.0 * jax.random.uniform(seeds[5], (HV,), jnp.float32) ** levels(seeds[5], (HV,), ((0, 4),), -0.2, 0.2), -2.0, 1.0),
        "dt_bias": jnp.clip(jax.random.uniform(seeds[6], (HV,), jnp.float32, -1.0, 1.0) * levels(seeds[6], (HV,), ((0, 4),), -0.4, 0.0), -1.0, 1.0),
        "norm_gain": jnp.clip(1.0 + 0.15 * jax.random.normal(seeds[7], (HEAD,), jnp.float32), 0.25, 1.75).astype(jnp.bfloat16),
        "w_out": gaussian_with(seeds[8], (HV * HEAD, D), (HV * HEAD) ** -0.5, 0.375, ((0, 4),), (0, 1, 4, 2.0)),
        "ffn_gain": jnp.clip(1.0 + 0.15 * jax.random.normal(seeds[9], (D,), jnp.float32), 0.25, 1.75).astype(jnp.bfloat16),
        "w_gu": scatter_about(seeds[10], (2, D, FF), D ** -0.5, 0.125, ((2, 4),)),
        "w_down": gaussian_with(seeds[11], (FF, D), FF ** -0.5, 0.125, ((0, 4),), (0, 1, 4, 2.0)),
        "state": scatter_about(part_splits[12], (SEQS, HV, HEAD, HEAD), 1.0, 6.0, ((0, 4), (1, 4)), jnp.float32),
        "conv_state": scatter_about(part_splits[13], (SEQS, KERNEL - 1, HV, 2 * HEAD), 1.0, 6.0, ((0, 4), (2, 4))),
    }


norm_eps = 1e-06
highest = lax.Precision.HIGHEST

def rounded(values):
    return lax.optimization_barrier(values.astype(jnp.bfloat16))

def rms_scaled(values, gain_vec):
    values = values.astype(jnp.float32)
    mean_square = lax.optimization_barrier(jnp.mean(values * values, axis=-1, keepdims=True))
    return values * lax.rsqrt(mean_square + norm_eps) * gain_vec.astype(jnp.float32)

def unit_rows(values):
    return values * lax.rsqrt(lax.optimization_barrier(jnp.sum(values * values, axis=-1, keepdims=True)) + norm_eps)

def reference(hidden, attn_gain, w_qkvz, w_ab, conv_weight, decay_log, dt_bias, norm_gain, w_out, ffn_gain, w_gu, w_down, state, conv_state):
    seq_count = hidden.shape[1]
    half_dim = HEAD // 2
    group_size = FF // HV
    out_heads = w_out.reshape(HV, HEAD, D)
    gate_groups = w_gu.reshape(2, D, HV, group_size).transpose(2, 0, 1, 3)
    down_groups = w_down.reshape(HV, group_size, D)
    carried = state
    window_state = conv_state
    outputs = []
    for step_num in range(STEPS):
        x_input = hidden[step_num]
        normed = rms_scaled(x_input, attn_gain).astype(jnp.bfloat16)
        projected = jnp.dot(normed, w_qkvz.reshape(D, -1), preferred_element_type=jnp.float32).reshape(seq_count, HV, 3 * HEAD)
        gate_in = jnp.dot(normed, w_ab.reshape(D, -1), preferred_element_type=jnp.float32).reshape(seq_count, HV, 2)
        mixed = rounded(projected[:, :, :2 * HEAD])
        window = jnp.concatenate([window_state, mixed[:, None]], axis=1)
        window_state = window[:, 1:]
        conv_sum = lax.optimization_barrier(jnp.sum(window.astype(jnp.float32) * conv_weight.astype(jnp.float32)[None], axis=1))
        conv_out = rounded(jax.nn.silu(conv_sum)).astype(jnp.float32)
        query_heads = conv_out[:, :, :half_dim].reshape(seq_count, HK, HEAD)
        key_heads = conv_out[:, :, half_dim:HEAD].reshape(seq_count, HK, HEAD)
        queries = jnp.repeat(unit_rows(query_heads) * HEAD ** (-0.5), 2, axis=1)
        key_vecs = jnp.repeat(unit_rows(key_heads), 2, axis=1)
        value_vecs = conv_out[:, :, HEAD:]
        alpha = jnp.exp(-jnp.exp(decay_log.astype(jnp.float32)) * jax.nn.softplus(gate_in[:, :, 0] + dt_bias.astype(jnp.float32)))
        beta = jax.nn.sigmoid(gate_in[:, :, 1])
        carried = carried * alpha[:, :, None, None]
        predicted = jnp.einsum('bhk,bhkv->bhv', key_vecs, carried, precision=highest)
        delta = (value_vecs - predicted) * beta[:, :, None]
        carried = carried + key_vecs[:, :, :, None] * delta[:, :, None, :]
        core = jnp.einsum('bhk,bhkv->bhv', queries, carried, precision=highest)
        gated = (rms_scaled(core, norm_gain) * jax.nn.silu(projected[:, :, 2 * HEAD:])).astype(jnp.bfloat16)

        def attend_term(total, pieces):
            head_rows, head_weight = pieces
            term = jnp.dot(head_rows, head_weight, preferred_element_type=jnp.float32)
            return (total + rounded(term).astype(jnp.float32), None)
        attention, _ = lax.scan(attend_term, jnp.zeros((seq_count, D), jnp.float32), (gated.transpose(1, 0, 2), out_heads))
        middle = rounded(x_input.astype(jnp.float32) + attention).astype(jnp.float32)
        normed_mid = rms_scaled(middle, ffn_gain).astype(jnp.bfloat16)

        def feed_term(total, pieces):
            pair_weights, down_rows = pieces
            gate_out = jnp.dot(normed_mid, pair_weights[0], preferred_element_type=jnp.float32)
            up_out = jnp.dot(normed_mid, pair_weights[1], preferred_element_type=jnp.float32)
            inner = (jax.nn.silu(gate_out) * up_out).astype(jnp.bfloat16)
            term = jnp.dot(inner, down_rows, preferred_element_type=jnp.float32)
            return (total + rounded(term).astype(jnp.float32), None)
        feed, _ = lax.scan(feed_term, jnp.zeros((seq_count, D), jnp.float32), (gate_groups, down_groups))
        outputs.append((middle + feed).astype(jnp.bfloat16))
    return (jnp.stack(outputs), carried, window_state)
```

```python
import functools

import jax
import jax.numpy as jnp
from jax import lax
from jax.experimental import pallas as pl
from jax.experimental.pallas import tpu as pltpu
from jax.sharding import PartitionSpec as P

D = 2048
HEAD = 128
STEPS = 2


norm_eps = 1e-06
highest = lax.Precision.HIGHEST
MESH = pl.DeviceIdType.MESH


def partner_2(block, axis, stride):
    count = lax.axis_size(axis)
    route = []
    for low in range(count):
        high = low | 1 << stride
        if high != low and high < count:
            route += [(low, high), (high, low)]
    return lax.ppermute(block, axis, route)


def rounded(values):
    return lax.optimization_barrier(values.astype(jnp.bfloat16))


def rms_scaled(values, gain_vec):
    values = values.astype(jnp.float32)
    mean_square = jnp.mean(values * values, axis=-1, keepdims=True)
    return values * lax.rsqrt(mean_square + norm_eps) * gain_vec.astype(jnp.float32)


def unit_rows(values):
    return values * lax.rsqrt(jnp.sum(values * values, axis=-1, keepdims=True) + norm_eps)


def reduce_terms(partial_value):
    term_bf = rounded(partial_value)
    return lax.psum_scatter(
        term_bf.astype(jnp.float32).astype(jnp.bfloat16), "tensor", scatter_dimension=1, tiled=True
    ).astype(jnp.float32)


def on_device(
    hidden,
    attn_gain,
    w_qkvz,
    w_ab,
    conv_weight,
    decay_log,
    dt_bias,
    norm_gain,
    w_out,
    ffn_gain,
    w_gu,
    w_down,
    state,
    conv_state,
):
    seq_count = hidden.shape[1]
    rank_here = lax.axis_index("tensor")
    half_dim = HEAD // 2
    is_odd = rank_here % 2 == 1
    carried = state
    window_state = conv_state
    outputs = []
    for step_num in range(STEPS):
        own_input = hidden[step_num]
        x_full = lax.all_gather(own_input, "tensor", axis=1, tiled=True)
        normed = rms_scaled(x_full, attn_gain).astype(jnp.bfloat16)
        projected = jnp.dot(
            normed, w_qkvz.reshape(D, -1), preferred_element_type=jnp.float32
        ).reshape(seq_count, 1, 3 * HEAD)
        gate_in = jnp.dot(normed, w_ab.reshape(D, -1), preferred_element_type=jnp.float32).reshape(
            seq_count, 1, 2
        )
        mixed = rounded(projected[:, :, : 2 * HEAD])
        window = jnp.concatenate([window_state, mixed[:, None]], axis=1)
        window_state = window[:, 1:]
        conv_sum = jnp.sum(
            window.astype(jnp.float32) * conv_weight.astype(jnp.float32)[None], axis=1
        )
        conv_bf = rounded(jax.nn.silu(conv_sum))
        own_halves = conv_bf[:, 0, :HEAD]
        partner = partner_2(own_halves, "tensor", 0)
        first_part = jnp.where(is_odd, partner, own_halves)
        second_part = jnp.where(is_odd, own_halves, partner)
        query_head = jnp.concatenate(
            [first_part[:, :half_dim], second_part[:, :half_dim]], axis=1
        ).astype(jnp.float32)
        key_head = jnp.concatenate(
            [first_part[:, half_dim:], second_part[:, half_dim:]], axis=1
        ).astype(jnp.float32)
        queries = (unit_rows(query_head) * HEAD ** (-0.5))[:, None]
        key_vecs = unit_rows(key_head)[:, None]
        value_vecs = conv_bf[:, :, HEAD:].astype(jnp.float32)
        alpha = jnp.exp(-jnp.exp(decay_log) * jax.nn.softplus(gate_in[:, :, 0] + dt_bias))
        beta = jax.nn.sigmoid(gate_in[:, :, 1])
        carried = carried * alpha[:, :, None, None]
        predicted = jnp.einsum("bhk,bhkv->bhv", key_vecs, carried, precision=highest)
        delta = (value_vecs - predicted) * beta[:, :, None]
        carried = carried + key_vecs[:, :, :, None] * delta[:, :, None, :]
        core = jnp.einsum("bhk,bhkv->bhv", queries, carried, precision=highest)
        gated = (rms_scaled(core, norm_gain) * jax.nn.silu(projected[:, :, 2 * HEAD :])).astype(
            jnp.bfloat16
        )
        partial_value = jnp.dot(
            gated.reshape(seq_count, HEAD), w_out, preferred_element_type=jnp.float32
        )
        attention = reduce_terms(partial_value)
        own_mid = rounded(own_input.astype(jnp.float32) + attention)
        middle = lax.all_gather(own_mid, "tensor", axis=1, tiled=True).astype(jnp.float32)
        middle_own = own_mid.astype(jnp.float32)
        normed_mid = rms_scaled(middle, ffn_gain).astype(jnp.bfloat16)
        gate_out = jnp.dot(normed_mid, w_gu[0], preferred_element_type=jnp.float32)
        up_out = jnp.dot(normed_mid, w_gu[1], preferred_element_type=jnp.float32)
        inner = (jax.nn.silu(gate_out) * up_out).astype(jnp.bfloat16)
        feed_partial = jnp.dot(inner, w_down, preferred_element_type=jnp.float32)
        feed_own = reduce_terms(feed_partial)
        outputs.append((middle_own + feed_own).astype(jnp.bfloat16))
    return (jnp.stack(outputs), carried, window_state)


def lane_tiles_fit(mesh, width, hidden_units):
    count = mesh.shape["tensor"]
    return count % 2 == 0 and width % (count * 128) == 0 and hidden_units % (count * 128) == 0


def sigmoid(values):
    return 1.0 / (1.0 + jnp.exp(-values))


def mixer_kernel(
    count,
    hidden,
    attn_gain,
    w_qkvz,
    w_ab,
    conv_weight,
    decay_log,
    dt_bias,
    norm_gain,
    w_out,
    ffn_gain,
    w_gu,
    w_down,
    state,
    conv_state,
    out_hidden,
    out_state,
    out_conv,
    x_all,
    qkvz,
    ab,
    taps,
    out_w,
    gu,
    down,
    carried,
    window,
    gains_in,
    head_gain,
    gains,
    split_state,
    vecs,
    products,
    decay,
    half_send,
    half_recv,
    att_send,
    att_recv,
    mid_all,
    feed_send,
    feed_recv,
    act,
    hidden_out,
    conv_out_buf,
    local_sem,
    x_sems,
    half_sems,
    att_sems,
    mid_sems,
    feed_sems,
):
    me = lax.axis_index("tensor")
    steps, seqs, width = hidden.shape
    rows = steps * seqs
    units = w_down.shape[0]
    f32, bf16 = jnp.float32, jnp.bfloat16

    def peer(index):
        pair = lax.rem(me // 2 + index // 2, count // 2)
        return 2 * pair + lax.rem(lax.rem(me, 2) + lax.rem(index, 2), 2)

    partner = peer(1)

    loads = []

    def load(src, dst):
        copy = pltpu.make_async_copy(src, dst, local_sem.at[len(loads)])
        copy.start()
        loads.append(copy)
        return copy

    load_x = [load(hidden.at[s], x_all.at[me, pl.ds(s * seqs, seqs)]) for s in range(steps)]
    load_gains = [load(attn_gain, gains_in.at[0]), load(ffn_gain, gains_in.at[1])]
    load_qkvz = [load(w_qkvz, qkvz), load(w_ab, ab)]
    load_state = load(state, carried)
    load_conv = [load(conv_weight, taps), load(conv_state, window)]
    load_norm = load(norm_gain, head_gain)
    load_out = load(w_out, out_w)
    load_gu = [load(w_gu.at[0], gu.at[0]), load(w_gu.at[1], gu.at[1])]
    load_down = load(w_down, down)

    barrier = pltpu.get_barrier_semaphore()
    for index in range(1, count):
        pl.semaphore_signal(
            barrier, inc=1, device_id={"tensor": peer(index)}, device_id_type=MESH
        )
    pl.semaphore_wait(barrier, count - 1)

    def remote(src, dst, send, recv, target):
        return pltpu.make_async_remote_copy(
            src_ref=src,
            dst_ref=dst,
            send_sem=send,
            recv_sem=recv,
            device_id={"tensor": target},
            device_id_type=MESH,
        )

    for copy in load_x:
        copy.wait()
    sends = []
    for index in reversed(range(1, count)):
        copy = remote(
            x_all.at[me], x_all.at[me], x_sems.at[0, index], x_sems.at[1, me], peer(index)
        )
        copy.start()
        sends.append(copy)

    for copy in load_gains:
        copy.wait()
    for which in range(2):
        for part in range(count):
            gains[which, part] = gains_in[which, :, pl.ds(part * width, width)].astype(f32)
    load_state.wait()

    @pl.loop(0, seqs)
    def _(seq):
        block = carried[seq]
        high = block.astype(bf16)
        split_state[seq, :HEAD] = high
        split_state[seq, HEAD:] = (block - high.astype(f32)).astype(bf16)

    for copy in load_qkvz:
        copy.wait()

    projected = jnp.zeros((rows, 3 * HEAD), f32)
    gate_in = jnp.zeros((rows, 2), f32)
    square = jnp.zeros((rows, 1), f32)
    for index in range(count):
        src = peer(index)
        if index:
            remote(
                x_all.at[src], x_all.at[src], x_sems.at[0, index], x_sems.at[1, src], src
            ).wait_recv()
        block = x_all[src].astype(f32)
        square += jnp.sum(block * block, axis=-1, keepdims=True)
        scaled = (block * gains[0, src]).astype(bf16)
        span = pl.ds(pl.multiple_of(src * width, width), width)
        projected += jnp.dot(scaled, qkvz[span, :], preferred_element_type=f32)
        gate_in += lax.dot_general(
            scaled, ab[:, span], (((1,), (1,)), ((), ())), preferred_element_type=f32
        )
    factor = lax.rsqrt(square / (count * width) + norm_eps)
    projected = projected * factor
    gate_in = gate_in * factor

    for copy in load_conv:
        copy.wait()
    mixed = projected[:, : 2 * HEAD].astype(bf16)
    kept = window.shape[0]
    for row in range(kept):
        place = row + steps - kept
        if place < 0:
            conv_out_buf[row] = window[row + steps]
        else:
            conv_out_buf[row] = mixed[place * seqs : (place + 1) * seqs]
    history = [window[row].astype(f32) for row in range(kept)]
    history += [mixed[s * seqs : (s + 1) * seqs].astype(f32) for s in range(steps)]
    tap_rows = taps[...].astype(f32)
    conv_steps = []
    for s in range(steps):
        total = history[s] * tap_rows[0:1]
        for tap in range(1, kept + 1):
            total += history[s + tap] * tap_rows[tap : tap + 1]
        conv_steps.append((total * sigmoid(total)).astype(bf16))
    conv_bf = jnp.concatenate(conv_steps, axis=0)
    half_send[...] = conv_bf[:, :HEAD]
    half_copy = remote(
        half_send, half_recv, half_sems.at[0], half_sems.at[1], partner
    )
    half_copy.start()
    store_conv = pltpu.make_async_copy(conv_out_buf, out_conv, local_sem.at[len(loads)])
    store_conv.start()

    shift = jnp.full((rows, 1), dt_bias[0], f32)
    rate = jnp.exp(jnp.full((rows, 1), decay_log[0], f32))
    biased = gate_in[:, 0:1] + shift
    softplus = jnp.maximum(biased, 0.0) + jnp.log1p(jnp.exp(-jnp.abs(biased)))
    alpha = jnp.exp(-rate * softplus)
    beta = sigmoid(gate_in[:, 1:2])
    out_gate = projected[:, 2 * HEAD :]
    out_gate = out_gate * sigmoid(out_gate)
    value_vecs = conv_bf[:, HEAD:].astype(f32)
    own = conv_bf[:, :HEAD].astype(f32)
    is_odd = lax.rem(me, 2) == 1
    low_lanes = lax.broadcasted_iota(jnp.int32, (rows, HEAD), 1) < HEAD // 2

    half_copy.wait_recv()
    other = half_recv[...].astype(f32)
    first = jnp.where(is_odd, other, own)
    second = jnp.where(is_odd, own, other)
    query_raw = jnp.where(low_lanes, first, pltpu.roll(second, HEAD // 2, 1))
    key_raw = jnp.where(low_lanes, pltpu.roll(first, HEAD // 2, 1), second)
    query_scale = lax.rsqrt(
        jnp.sum(query_raw * query_raw, axis=-1, keepdims=True) + norm_eps
    ) * HEAD ** (-0.5)
    key_scale = lax.rsqrt(jnp.sum(key_raw * key_raw, axis=-1, keepdims=True) + norm_eps)

    for s in range(steps):
        part = slice(s * seqs, (s + 1) * seqs)
        vecs[:, 2 * s, :] = key_raw[part]
        vecs[:, 2 * s + 1, :] = query_raw[part]
    for row in range(2 * steps, 8):
        vecs[:, row, :] = jnp.zeros((seqs, HEAD), f32)

    group = 8

    @pl.loop(0, seqs // group)
    def _(outer):
        for inner_seq in range(group):
            seq = outer * group + inner_seq
            lhs = vecs[seq].astype(bf16)
            products[seq] = jnp.dot(
                jnp.concatenate([lhs, lhs], axis=1),
                split_state[seq],
                preferred_element_type=f32,
            )

    queries = query_raw * query_scale
    key_vecs = key_raw * key_scale
    cut = [slice(s * seqs, (s + 1) * seqs) for s in range(steps)]
    deltas, cores = [], []
    total_decay = jnp.ones((seqs, 1), f32)
    for s in range(steps):
        a = alpha[cut[s]]
        total_decay = total_decay * a
        predicted = products[:, 2 * s, :] * (key_scale[cut[s]] * total_decay)
        read = products[:, 2 * s + 1, :] * (query_scale[cut[s]] * total_decay)
        deltas = [d * a for d in deltas]
        for t in range(s):
            predicted += deltas[t] * jnp.sum(
                key_vecs[cut[s]] * key_vecs[cut[t]], axis=-1, keepdims=True
            )
            read += deltas[t] * jnp.sum(
                queries[cut[s]] * key_vecs[cut[t]], axis=-1, keepdims=True
            )
        delta = (value_vecs[cut[s]] - predicted) * beta[cut[s]]
        read += delta * jnp.sum(queries[cut[s]] * key_vecs[cut[s]], axis=-1, keepdims=True)
        deltas.append(delta)
        cores.append(read)
    core = jnp.concatenate(cores, axis=0)
    load_norm.wait()
    core_factor = lax.rsqrt(jnp.mean(core * core, axis=-1, keepdims=True) + norm_eps)
    gated = (core * core_factor * head_gain[...].astype(f32) * out_gate).astype(bf16)

    load_out.wait()
    for index in reversed(range(count)):
        target = peer(index)
        span = pl.ds(pl.multiple_of(target * width, width), width)
        term = jnp.dot(gated, out_w[:, span], preferred_element_type=f32).astype(bf16)
        if index == 0:
            attention = term.astype(f32)
        else:
            att_send[index] = term
            copy = remote(
                att_send.at[index], att_recv.at[me], att_sems.at[0, index], att_sems.at[1, me], target
            )
            copy.start()
            sends.append(copy)

    decay[...] = jnp.broadcast_to(total_decay, (seqs, HEAD))
    for s in range(steps):
        written = deltas[s] * key_scale[cut[s]]
        high = written.astype(bf16).astype(f32)
        vecs[:, 4 * s // 2, :] = key_raw[cut[s]]
        vecs[:, 4 * s // 2 + 1, :] = key_raw[cut[s]]
        products[:, 2 * s, :] = high
        products[:, 2 * s + 1, :] = written - high
    for row in range(2 * steps, 8):
        products[:, row, :] = jnp.zeros((seqs, HEAD), f32)

    @pl.loop(0, seqs // group)
    def _(outer):
        for inner_seq in range(group):
            seq = outer * group + inner_seq
            columns = jnp.transpose(vecs[seq]).astype(bf16)
            carried[seq] = carried[seq] * decay[pl.ds(seq, 1), :] + jnp.dot(
                columns, products[seq].astype(bf16), preferred_element_type=f32
            )

    store_state = pltpu.make_async_copy(carried, out_state, local_sem.at[len(loads) + 1])
    store_state.start()

    for index in range(1, count):
        src = peer(index)
        remote(
            att_send.at[index], att_recv.at[src], att_sems.at[0, index], att_sems.at[1, src], src
        ).wait_recv()
        attention += att_recv[src].astype(f32)
    mid_own = (x_all[me].astype(f32) + attention).astype(bf16)
    mid_all[me] = mid_own
    for index in reversed(range(1, count)):
        copy = remote(
            mid_all.at[me], mid_all.at[me], mid_sems.at[0, index], mid_sems.at[1, me], peer(index)
        )
        copy.start()
        sends.append(copy)

    for copy in load_gu:
        copy.wait()
    square = jnp.zeros((rows, 1), f32)
    for index in range(count):
        src = peer(index)
        if index:
            remote(
                mid_all.at[src], mid_all.at[src], mid_sems.at[0, index], mid_sems.at[1, src], src
            ).wait_recv()
        block = mid_all[src].astype(f32)
        square += jnp.sum(block * block, axis=-1, keepdims=True)
        scaled = (block * gains[1, src]).astype(bf16)
        span = pl.ds(pl.multiple_of(src * width, width), width)
        for which in range(2):
            term = jnp.dot(scaled, gu[which, span, :], preferred_element_type=f32)
            if index == 0:
                act[which] = term
            else:
                act[which] += term
    factor = lax.rsqrt(square / (count * width) + norm_eps)
    gate_out = act[0] * factor
    inner = (gate_out * sigmoid(gate_out) * (act[1] * factor)).astype(bf16)

    load_down.wait()
    for index in reversed(range(count)):
        target = peer(index)
        span = pl.ds(pl.multiple_of(target * width, width), width)
        term = jnp.dot(inner, down[:, span], preferred_element_type=f32).astype(bf16)
        if index == 0:
            feed = term.astype(f32)
        else:
            feed_send[index] = term
            copy = remote(
                feed_send.at[index], feed_recv.at[me], feed_sems.at[0, index], feed_sems.at[1, me], target
            )
            copy.start()
            sends.append(copy)
    for index in range(1, count):
        src = peer(index)
        remote(
            feed_send.at[index], feed_recv.at[src], feed_sems.at[0, index], feed_sems.at[1, src], src
        ).wait_recv()
        feed += feed_recv[src].astype(f32)
    final = (mid_all[me].astype(f32) + feed).astype(bf16)
    for s in range(steps):
        hidden_out[s] = final[cut[s]]
    store_hidden = pltpu.make_async_copy(hidden_out, out_hidden, local_sem.at[len(loads) + 2])
    store_hidden.start()
    half_copy.wait_send()
    for copy in sends:
        copy.wait_send()
    store_conv.wait()
    store_state.wait()
    store_hidden.wait()


def in_one_kernel(
    hidden,
    attn_gain,
    w_qkvz,
    w_ab,
    conv_weight,
    decay_log,
    dt_bias,
    norm_gain,
    w_out,
    ffn_gain,
    w_gu,
    w_down,
    state,
    conv_state,
):
    count = lax.axis_size("tensor")
    steps, seqs, width = hidden.shape
    rows, full, units = steps * seqs, count * width, w_down.shape[0]
    kept = conv_state.shape[1]
    f32, bf16 = jnp.float32, jnp.bfloat16
    anywhere = pl.BlockSpec(memory_space=pl.ANY)
    scalar = pl.BlockSpec(memory_space=pltpu.SMEM)
    in_specs = [anywhere] * 5 + [scalar] * 2 + [anywhere] * 7
    vmem = pltpu.VMEM
    pair = pltpu.SemaphoreType.DMA((2, count))
    out = pl.pallas_call(
        functools.partial(mixer_kernel, count),
        out_shape=(
            jax.ShapeDtypeStruct(hidden.shape, bf16),
            jax.ShapeDtypeStruct((seqs, HEAD, HEAD), f32),
            jax.ShapeDtypeStruct((kept, seqs, 2 * HEAD), bf16),
        ),
        in_specs=in_specs,
        out_specs=(anywhere,) * 3,
        scratch_shapes=[
            vmem((count, rows, width), bf16),
            vmem((full, 3 * HEAD), bf16),
            vmem((2, full), bf16),
            vmem((kept + 1, 2 * HEAD), bf16),
            vmem((HEAD, full), bf16),
            vmem((2, full, units), bf16),
            vmem((units, full), bf16),
            vmem((seqs, HEAD, HEAD), f32),
            vmem((kept, seqs, 2 * HEAD), bf16),
            vmem((2, 1, full), bf16),
            vmem((1, HEAD), bf16),
            vmem((2, count, 1, width), f32),
            vmem((seqs, 2 * HEAD, HEAD), bf16),
            vmem((seqs, 8, HEAD), f32),
            vmem((seqs, 8, HEAD), f32),
            vmem((seqs, HEAD), f32),
            vmem((rows, HEAD), bf16),
            vmem((rows, HEAD), bf16),
            vmem((count, rows, width), bf16),
            vmem((count, rows, width), bf16),
            vmem((count, rows, width), bf16),
            vmem((count, rows, width), bf16),
            vmem((count, rows, width), bf16),
            vmem((2, rows, units), f32),
            vmem(hidden.shape, bf16),
            vmem((kept, seqs, 2 * HEAD), bf16),
            pltpu.SemaphoreType.DMA((20,)),
            pair,
            pltpu.SemaphoreType.DMA((2,)),
            pair,
            pair,
            pair,
        ],
        compiler_params=pltpu.CompilerParams(
            collective_id=0, has_side_effects=True, vmem_limit_bytes=44 * 2**20
        ),
    )(
        hidden,
        attn_gain.reshape(1, full),
        w_qkvz.reshape(full, 3 * HEAD),
        w_ab.reshape(full, 2).T,
        conv_weight.reshape(kept + 1, 2 * HEAD),
        decay_log,
        dt_bias,
        norm_gain.reshape(1, HEAD),
        w_out,
        ffn_gain.reshape(1, full),
        w_gu,
        w_down,
        state.reshape(seqs, HEAD, HEAD),
        conv_state.reshape(seqs, kept, 2 * HEAD).transpose(1, 0, 2),
    )
    next_hidden, next_state, next_conv = out
    return (
        next_hidden,
        next_state[:, None],
        next_conv.transpose(1, 0, 2)[:, :, None],
    )


def solution(mesh):
    placed = (
        P(None, ("groups", "dp"), "tensor"),
        P(),
        P(None, "tensor", None),
        P(None, "tensor", None),
        P(None, "tensor", None),
        P("tensor"),
        P("tensor"),
        P(),
        P("tensor", None),
        P(),
        P(None, None, "tensor"),
        P("tensor", None),
        P(("groups", "dp"), "tensor", None, None),
        P(("groups", "dp"), None, "tensor", None),
    )
    out_placed = (placed[0], placed[12], placed[13])

    def whole(*args):
        fits = lane_tiles_fit(mesh, args[0].shape[2], args[11].shape[0])
        one_head = args[2].shape[1] == mesh.shape["tensor"]
        body = in_one_kernel if fits and one_head else on_device
        return jax.shard_map(
            body, mesh=mesh, in_specs=placed, out_specs=out_placed, check_vma=False
        )(*args)

    return whole
```

```python
import functools

import jax
import jax.numpy as jnp
from jax import lax
from jax.experimental import pallas as pl
from jax.experimental.pallas import tpu as pltpu
from jax.sharding import PartitionSpec as P

D = 2048
HEAD = 128
STEPS = 2


norm_eps = 1e-06
highest = lax.Precision.HIGHEST
MESH = pl.DeviceIdType.MESH


def partner_2(block, axis, stride):
    count = lax.axis_size(axis)
    route = []
    for low in range(count):
        high = low | 1 << stride
        if high != low and high < count:
            route += [(low, high), (high, low)]
    return lax.ppermute(block, axis, route)


def rounded(values):
    return lax.optimization_barrier(values.astype(jnp.bfloat16))


def rms_scaled(values, gain_vec):
    values = values.astype(jnp.float32)
    mean_square = jnp.mean(values * values, axis=-1, keepdims=True)
    return values * lax.rsqrt(mean_square + norm_eps) * gain_vec.astype(jnp.float32)


def unit_rows(values):
    return values * lax.rsqrt(jnp.sum(values * values, axis=-1, keepdims=True) + norm_eps)


def reduce_terms(partial_value):
    term_bf = rounded(partial_value)
    return lax.psum_scatter(
        term_bf.astype(jnp.float32).astype(jnp.bfloat16), "tensor", scatter_dimension=1, tiled=True
    ).astype(jnp.float32)


def on_device(
    hidden,
    attn_gain,
    w_qkvz,
    w_ab,
    conv_weight,
    decay_log,
    dt_bias,
    norm_gain,
    w_out,
    ffn_gain,
    w_gu,
    w_down,
    state,
    conv_state,
):
    seq_count = hidden.shape[1]
    rank_here = lax.axis_index("tensor")
    half_dim = HEAD // 2
    is_odd = rank_here % 2 == 1
    carried = state
    window_state = conv_state
    outputs = []
    for step_num in range(STEPS):
        own_input = hidden[step_num]
        x_full = lax.all_gather(own_input, "tensor", axis=1, tiled=True)
        normed = rms_scaled(x_full, attn_gain).astype(jnp.bfloat16)
        projected = jnp.dot(
            normed, w_qkvz.reshape(D, -1), preferred_element_type=jnp.float32
        ).reshape(seq_count, 1, 3 * HEAD)
        gate_in = jnp.dot(normed, w_ab.reshape(D, -1), preferred_element_type=jnp.float32).reshape(
            seq_count, 1, 2
        )
        mixed = rounded(projected[:, :, : 2 * HEAD])
        window = jnp.concatenate([window_state, mixed[:, None]], axis=1)
        window_state = window[:, 1:]
        conv_sum = jnp.sum(
            window.astype(jnp.float32) * conv_weight.astype(jnp.float32)[None], axis=1
        )
        conv_bf = rounded(jax.nn.silu(conv_sum))
        own_halves = conv_bf[:, 0, :HEAD]
        partner = partner_2(own_halves, "tensor", 0)
        first_part = jnp.where(is_odd, partner, own_halves)
        second_part = jnp.where(is_odd, own_halves, partner)
        query_head = jnp.concatenate(
            [first_part[:, :half_dim], second_part[:, :half_dim]], axis=1
        ).astype(jnp.float32)
        key_head = jnp.concatenate(
            [first_part[:, half_dim:], second_part[:, half_dim:]], axis=1
        ).astype(jnp.float32)
        queries = (unit_rows(query_head) * HEAD ** (-0.5))[:, None]
        key_vecs = unit_rows(key_head)[:, None]
        value_vecs = conv_bf[:, :, HEAD:].astype(jnp.float32)
        alpha = jnp.exp(-jnp.exp(decay_log) * jax.nn.softplus(gate_in[:, :, 0] + dt_bias))
        beta = jax.nn.sigmoid(gate_in[:, :, 1])
        carried = carried * alpha[:, :, None, None]
        predicted = jnp.einsum("bhk,bhkv->bhv", key_vecs, carried, precision=highest)
        delta = (value_vecs - predicted) * beta[:, :, None]
        carried = carried + key_vecs[:, :, :, None] * delta[:, :, None, :]
        core = jnp.einsum("bhk,bhkv->bhv", queries, carried, precision=highest)
        gated = (rms_scaled(core, norm_gain) * jax.nn.silu(projected[:, :, 2 * HEAD :])).astype(
            jnp.bfloat16
        )
        partial_value = jnp.dot(
            gated.reshape(seq_count, HEAD), w_out, preferred_element_type=jnp.float32
        )
        attention = reduce_terms(partial_value)
        own_mid = rounded(own_input.astype(jnp.float32) + attention)
        middle = lax.all_gather(own_mid, "tensor", axis=1, tiled=True).astype(jnp.float32)
        middle_own = own_mid.astype(jnp.float32)
        normed_mid = rms_scaled(middle, ffn_gain).astype(jnp.bfloat16)
        gate_out = jnp.dot(normed_mid, w_gu[0], preferred_element_type=jnp.float32)
        up_out = jnp.dot(normed_mid, w_gu[1], preferred_element_type=jnp.float32)
        inner = (jax.nn.silu(gate_out) * up_out).astype(jnp.bfloat16)
        feed_partial = jnp.dot(inner, w_down, preferred_element_type=jnp.float32)
        feed_own = reduce_terms(feed_partial)
        outputs.append((middle_own + feed_own).astype(jnp.bfloat16))
    return (jnp.stack(outputs), carried, window_state)


def lane_tiles_fit(mesh, width, hidden_units):
    count = mesh.shape["tensor"]
    return count % 2 == 0 and width % (count * 128) == 0 and hidden_units % (count * 128) == 0


def sigmoid(values):
    return 1.0 / (1.0 + jnp.exp(-values))


def mixer_kernel(
    count,
    hidden,
    attn_gain,
    w_qkvz,
    w_ab,
    conv_weight,
    decay_log,
    dt_bias,
    norm_gain,
    w_out,
    ffn_gain,
    w_gu,
    w_down,
    state,
    conv_state,
    out_hidden,
    out_state,
    out_conv,
    x_all,
    qkvz,
    ab,
    taps,
    out_w,
    gu,
    down,
    carried,
    window,
    gains_in,
    head_gain,
    gains,
    split_state,
    vecs,
    products,
    decay,
    half_send,
    half_recv,
    att_send,
    att_recv,
    mid_all,
    feed_send,
    feed_recv,
    act,
    hidden_out,
    conv_out_buf,
    local_sem,
    x_sems,
    half_sems,
    att_sems,
    mid_sems,
    feed_sems,
):
    me = lax.axis_index("tensor")
    steps, seqs, width = hidden.shape
    rows = steps * seqs
    units = w_down.shape[0]
    f32, bf16 = jnp.float32, jnp.bfloat16

    def peer(index):
        pair = lax.rem(me // 2 + index // 2, count // 2)
        return 2 * pair + lax.rem(lax.rem(me, 2) + lax.rem(index, 2), 2)

    partner = peer(1)

    loads = []

    def load(src, dst):
        copy = pltpu.make_async_copy(src, dst, local_sem.at[len(loads)])
        copy.start()
        loads.append(copy)
        return copy

    load_x = [load(hidden.at[s], x_all.at[me, pl.ds(s * seqs, seqs)]) for s in range(steps)]
    load_gains = [load(attn_gain, gains_in.at[0]), load(ffn_gain, gains_in.at[1])]
    load_qkvz = [load(w_qkvz, qkvz), load(w_ab, ab)]
    load_state = load(state, carried)
    load_conv = [load(conv_weight, taps), load(conv_state, window)]
    load_norm = load(norm_gain, head_gain)
    load_out = load(w_out, out_w)
    load_gu = [load(w_gu.at[0], gu.at[0]), load(w_gu.at[1], gu.at[1])]
    load_down = load(w_down, down)

    barrier = pltpu.get_barrier_semaphore()
    for index in range(1, count):
        pl.semaphore_signal(
            barrier, inc=1, device_id={"tensor": peer(index)}, device_id_type=MESH
        )
    pl.semaphore_wait(barrier, count - 1)

    def remote(src, dst, send, recv, target):
        return pltpu.make_async_remote_copy(
            src_ref=src,
            dst_ref=dst,
            send_sem=send,
            recv_sem=recv,
            device_id={"tensor": target},
            device_id_type=MESH,
        )

    for copy in load_x:
        copy.wait()
    sends = []
    for index in reversed(range(1, count)):
        copy = remote(
            x_all.at[me], x_all.at[me], x_sems.at[0, index], x_sems.at[1, me], peer(index)
        )
        copy.start()
        sends.append(copy)

    for copy in load_gains:
        copy.wait()
    for which in range(2):
        for part in range(count):
            for tile in range(width // 128):
                row = part * (width // 128) + tile
                gains[which, part, :, tile * 128 : (tile + 1) * 128] = gains_in[
                    which, row : row + 1, :
                ].astype(f32)
    load_state.wait()

    @pl.loop(0, seqs)
    def _(seq):
        block = carried[seq]
        high = block.astype(bf16)
        split_state[seq, :HEAD] = high
        split_state[seq, HEAD:] = (block - high.astype(f32)).astype(bf16)

    for copy in load_qkvz:
        copy.wait()

    projected = jnp.zeros((rows, 3 * HEAD), f32)
    gate_in = jnp.zeros((rows, 2), f32)
    square = jnp.zeros((rows, 1), f32)
    for index in range(count):
        src = peer(index)
        if index:
            remote(
                x_all.at[src], x_all.at[src], x_sems.at[0, index], x_sems.at[1, src], src
            ).wait_recv()
        block = x_all[src].astype(f32)
        square += jnp.sum(block * block, axis=-1, keepdims=True)
        scaled = (block * gains[0, src]).astype(bf16)
        span = pl.ds(pl.multiple_of(src * width, width), width)
        projected += jnp.dot(scaled, qkvz[span, :], preferred_element_type=f32)
        gate_in += lax.dot_general(
            scaled, ab[:, span], (((1,), (1,)), ((), ())), preferred_element_type=f32
        )
    factor = lax.rsqrt(square / (count * width) + norm_eps)
    projected = projected * factor
    gate_in = gate_in * factor

    for copy in load_conv:
        copy.wait()
    mixed = projected[:, : 2 * HEAD].astype(bf16)
    kept = window.shape[0]
    for row in range(kept):
        place = row + steps - kept
        if place < 0:
            conv_out_buf[row] = window[row + steps]
        else:
            conv_out_buf[row] = mixed[place * seqs : (place + 1) * seqs]
    history = [window[row].astype(f32) for row in range(kept)]
    history += [mixed[s * seqs : (s + 1) * seqs].astype(f32) for s in range(steps)]
    tap_rows = taps[...].astype(f32)
    conv_steps = []
    for s in range(steps):
        total = history[s] * tap_rows[0:1]
        for tap in range(1, kept + 1):
            total += history[s + tap] * tap_rows[tap : tap + 1]
        conv_steps.append((total * sigmoid(total)).astype(bf16))
    conv_bf = jnp.concatenate(conv_steps, axis=0)
    half_send[...] = conv_bf[:, :HEAD]
    half_copy = remote(
        half_send, half_recv, half_sems.at[0], half_sems.at[1], partner
    )
    half_copy.start()
    store_conv = pltpu.make_async_copy(conv_out_buf, out_conv, local_sem.at[len(loads)])
    store_conv.start()

    shift = jnp.full((rows, 1), dt_bias[0], f32)
    rate = jnp.exp(jnp.full((rows, 1), decay_log[0], f32))
    biased = gate_in[:, 0:1] + shift
    softplus = jnp.maximum(biased, 0.0) + jnp.log1p(jnp.exp(-jnp.abs(biased)))
    alpha = jnp.exp(-rate * softplus)
    beta = sigmoid(gate_in[:, 1:2])
    out_gate = projected[:, 2 * HEAD :]
    out_gate = out_gate * sigmoid(out_gate)
    value_vecs = conv_bf[:, HEAD:].astype(f32)
    own = conv_bf[:, :HEAD].astype(f32)
    is_odd = lax.rem(me, 2) == 1
    low_lanes = lax.broadcasted_iota(jnp.int32, (rows, HEAD), 1) < HEAD // 2

    half_copy.wait_recv()
    other = half_recv[...].astype(f32)
    first = jnp.where(is_odd, other, own)
    second = jnp.where(is_odd, own, other)
    query_raw = jnp.where(low_lanes, first, pltpu.roll(second, HEAD // 2, 1))
    key_raw = jnp.where(low_lanes, pltpu.roll(first, HEAD // 2, 1), second)
    query_scale = lax.rsqrt(
        jnp.sum(query_raw * query_raw, axis=-1, keepdims=True) + norm_eps
    ) * HEAD ** (-0.5)
    key_scale = lax.rsqrt(jnp.sum(key_raw * key_raw, axis=-1, keepdims=True) + norm_eps)

    for s in range(steps):
        part = slice(s * seqs, (s + 1) * seqs)
        vecs[:, 2 * s, :] = key_raw[part]
        vecs[:, 2 * s + 1, :] = query_raw[part]
    for row in range(2 * steps, 8):
        vecs[:, row, :] = jnp.zeros((seqs, HEAD), f32)

    group = 8

    @pl.loop(0, seqs // group)
    def _(outer):
        for inner_seq in range(group):
            seq = outer * group + inner_seq
            lhs = vecs[seq].astype(bf16)
            products[seq] = jnp.dot(
                jnp.concatenate([lhs, lhs], axis=1),
                split_state[seq],
                preferred_element_type=f32,
            )

    queries = query_raw * query_scale
    key_vecs = key_raw * key_scale
    cut = [slice(s * seqs, (s + 1) * seqs) for s in range(steps)]
    deltas, cores = [], []
    total_decay = jnp.ones((seqs, 1), f32)
    for s in range(steps):
        a = alpha[cut[s]]
        total_decay = total_decay * a
        predicted = products[:, 2 * s, :] * (key_scale[cut[s]] * total_decay)
        read = products[:, 2 * s + 1, :] * (query_scale[cut[s]] * total_decay)
        deltas = [d * a for d in deltas]
        for t in range(s):
            predicted += deltas[t] * jnp.sum(
                key_vecs[cut[s]] * key_vecs[cut[t]], axis=-1, keepdims=True
            )
            read += deltas[t] * jnp.sum(
                queries[cut[s]] * key_vecs[cut[t]], axis=-1, keepdims=True
            )
        delta = (value_vecs[cut[s]] - predicted) * beta[cut[s]]
        read += delta * jnp.sum(queries[cut[s]] * key_vecs[cut[s]], axis=-1, keepdims=True)
        deltas.append(delta)
        cores.append(read)
    core = jnp.concatenate(cores, axis=0)
    load_norm.wait()
    core_factor = lax.rsqrt(jnp.mean(core * core, axis=-1, keepdims=True) + norm_eps)
    gated = (core * core_factor * head_gain[...].astype(f32) * out_gate).astype(bf16)

    load_out.wait()
    for index in reversed(range(count)):
        target = peer(index)
        span = pl.ds(pl.multiple_of(target * width, width), width)
        term = jnp.dot(gated, out_w[:, span], preferred_element_type=f32).astype(bf16)
        if index == 0:
            attention = term.astype(f32)
        else:
            att_send[index] = term
            copy = remote(
                att_send.at[index], att_recv.at[me], att_sems.at[0, index], att_sems.at[1, me], target
            )
            copy.start()
            sends.append(copy)

    decay[...] = jnp.broadcast_to(total_decay, (seqs, HEAD))
    for s in range(steps):
        written = deltas[s] * key_scale[cut[s]]
        high = written.astype(bf16).astype(f32)
        vecs[:, 4 * s // 2, :] = key_raw[cut[s]]
        vecs[:, 4 * s // 2 + 1, :] = key_raw[cut[s]]
        products[:, 2 * s, :] = high
        products[:, 2 * s + 1, :] = written - high
    for row in range(2 * steps, 8):
        products[:, row, :] = jnp.zeros((seqs, HEAD), f32)

    @pl.loop(0, seqs // group)
    def _(outer):
        for inner_seq in range(group):
            seq = outer * group + inner_seq
            columns = jnp.transpose(vecs[seq]).astype(bf16)
            carried[seq] = carried[seq] * decay[pl.ds(seq, 1), :] + jnp.dot(
                columns, products[seq].astype(bf16), preferred_element_type=f32
            )

    store_state = pltpu.make_async_copy(carried, out_state, local_sem.at[len(loads) + 1])
    store_state.start()

    for index in range(1, count):
        src = peer(index)
        remote(
            att_send.at[index], att_recv.at[src], att_sems.at[0, index], att_sems.at[1, src], src
        ).wait_recv()
        attention += att_recv[src].astype(f32)
    mid_own = (x_all[me].astype(f32) + attention).astype(bf16)
    mid_all[me] = mid_own
    for index in reversed(range(1, count)):
        copy = remote(
            mid_all.at[me], mid_all.at[me], mid_sems.at[0, index], mid_sems.at[1, me], peer(index)
        )
        copy.start()
        sends.append(copy)

    for copy in load_gu:
        copy.wait()
    square = jnp.zeros((rows, 1), f32)
    for index in range(count):
        src = peer(index)
        if index:
            remote(
                mid_all.at[src], mid_all.at[src], mid_sems.at[0, index], mid_sems.at[1, src], src
            ).wait_recv()
        block = mid_all[src].astype(f32)
        square += jnp.sum(block * block, axis=-1, keepdims=True)
        scaled = (block * gains[1, src]).astype(bf16)
        span = pl.ds(pl.multiple_of(src * width, width), width)
        for which in range(2):
            term = jnp.dot(scaled, gu[which, span, :], preferred_element_type=f32)
            if index == 0:
                act[which] = term
            else:
                act[which] += term
    factor = lax.rsqrt(square / (count * width) + norm_eps)
    gate_out = act[0] * factor
    inner = (gate_out * sigmoid(gate_out) * (act[1] * factor)).astype(bf16)

    load_down.wait()
    for index in reversed(range(count)):
        target = peer(index)
        span = pl.ds(pl.multiple_of(target * width, width), width)
        term = jnp.dot(inner, down[:, span], preferred_element_type=f32).astype(bf16)
        if index == 0:
            feed = term.astype(f32)
        else:
            feed_send[index] = term
            copy = remote(
                feed_send.at[index], feed_recv.at[me], feed_sems.at[0, index], feed_sems.at[1, me], target
            )
            copy.start()
            sends.append(copy)
    for index in range(1, count):
        src = peer(index)
        remote(
            feed_send.at[index], feed_recv.at[src], feed_sems.at[0, index], feed_sems.at[1, src], src
        ).wait_recv()
        feed += feed_recv[src].astype(f32)
    final = (mid_all[me].astype(f32) + feed).astype(bf16)
    for s in range(steps):
        hidden_out[s] = final[cut[s]]
    store_hidden = pltpu.make_async_copy(hidden_out, out_hidden, local_sem.at[len(loads) + 2])
    store_hidden.start()
    half_copy.wait_send()
    for copy in sends:
        copy.wait_send()
    store_conv.wait()
    store_state.wait()
    store_hidden.wait()


def finish_kernel(*refs):
    sources, targets, sems = refs[:3], refs[3:6], refs[6]
    copies = []
    for source, target in zip(sources, targets):
        cuts = 4 if source.shape[0] % 4 == 0 else 1
        size = source.shape[0] // cuts
        for cut in range(cuts):
            span = pl.ds(cut * size, size)
            copies.append(
                pltpu.make_async_copy(source.at[span], target.at[span], sems.at[len(copies)])
            )
    for copy in copies:
        copy.start()
    for copy in copies:
        copy.wait()


def in_one_kernel(
    hidden,
    attn_gain,
    w_qkvz,
    w_ab,
    conv_weight,
    decay_log,
    dt_bias,
    norm_gain,
    w_out,
    ffn_gain,
    w_gu,
    w_down,
    state,
    conv_state,
):
    count = lax.axis_size("tensor")
    steps, seqs, width = hidden.shape
    rows, full, units = steps * seqs, count * width, w_down.shape[0]
    kept = conv_state.shape[1]
    f32, bf16 = jnp.float32, jnp.bfloat16
    anywhere = pl.BlockSpec(memory_space=pl.ANY)
    scalar = pl.BlockSpec(memory_space=pltpu.SMEM)
    in_hbm = pl.BlockSpec(memory_space=pltpu.HBM)
    in_specs = [in_hbm] * 5 + [scalar] * 2 + [in_hbm] * 7
    vmem = pltpu.VMEM
    pair = pltpu.SemaphoreType.DMA((2, count))
    out = pl.pallas_call(
        functools.partial(mixer_kernel, count),
        out_shape=(
            jax.ShapeDtypeStruct(hidden.shape, bf16),
            jax.ShapeDtypeStruct((seqs, HEAD, HEAD), f32),
            jax.ShapeDtypeStruct((kept, seqs, 2 * HEAD), bf16),
        ),
        in_specs=in_specs,
        out_specs=(anywhere,) * 3,
        scratch_shapes=[
            vmem((count, rows, width), bf16),
            vmem((full, 3 * HEAD), bf16),
            vmem((2, full), bf16),
            vmem((kept + 1, 2 * HEAD), bf16),
            vmem((HEAD, full), bf16),
            vmem((2, full, units), bf16),
            vmem((units, full), bf16),
            vmem((seqs, HEAD, HEAD), f32),
            vmem((kept, seqs, 2 * HEAD), bf16),
            vmem((2, full // 128, 128), bf16),
            vmem((1, HEAD), bf16),
            vmem((2, count, 1, width), f32),
            vmem((seqs, 2 * HEAD, HEAD), bf16),
            vmem((seqs, 8, HEAD), f32),
            vmem((seqs, 8, HEAD), f32),
            vmem((seqs, HEAD), f32),
            vmem((rows, HEAD), bf16),
            vmem((rows, HEAD), bf16),
            vmem((count, rows, width), bf16),
            vmem((count, rows, width), bf16),
            vmem((count, rows, width), bf16),
            vmem((count, rows, width), bf16),
            vmem((count, rows, width), bf16),
            vmem((2, rows, units), f32),
            vmem(hidden.shape, bf16),
            vmem((kept, seqs, 2 * HEAD), bf16),
            pltpu.SemaphoreType.DMA((20,)),
            pair,
            pltpu.SemaphoreType.DMA((2,)),
            pair,
            pair,
            pair,
        ],
        compiler_params=pltpu.CompilerParams(
            collective_id=0, has_side_effects=True, vmem_limit_bytes=63 * 2**20
        ),
    )(
        hidden,
        attn_gain.reshape(full // 128, 128),
        w_qkvz.reshape(full, 3 * HEAD),
        w_ab.reshape(full, 2).T,
        conv_weight.reshape(kept + 1, 2 * HEAD),
        decay_log,
        dt_bias,
        norm_gain.reshape(1, HEAD),
        w_out,
        ffn_gain.reshape(full // 128, 128),
        w_gu,
        w_down,
        state.reshape(seqs, HEAD, HEAD),
        conv_state.reshape(seqs, kept, 2 * HEAD).transpose(1, 0, 2),
    )
    next_hidden, next_state, next_conv = pl.pallas_call(
        finish_kernel,
        out_shape=tuple(jax.ShapeDtypeStruct(a.shape, a.dtype) for a in out),
        in_specs=[anywhere] * 3,
        out_specs=(anywhere,) * 3,
        scratch_shapes=[pltpu.SemaphoreType.DMA((12,))],
    )(*out)
    return (
        next_hidden,
        next_state[:, None],
        next_conv.transpose(1, 0, 2)[:, :, None],
    )


def solution(mesh):
    placed = (
        P(None, ("groups", "dp"), "tensor"),
        P(),
        P(None, "tensor", None),
        P(None, "tensor", None),
        P(None, "tensor", None),
        P("tensor"),
        P("tensor"),
        P(),
        P("tensor", None),
        P(),
        P(None, None, "tensor"),
        P("tensor", None),
        P(("groups", "dp"), "tensor", None, None),
        P(("groups", "dp"), None, "tensor", None),
    )
    out_placed = (placed[0], placed[12], placed[13])

    def whole(*args):
        fits = lane_tiles_fit(mesh, args[0].shape[2], args[11].shape[0])
        one_head = args[2].shape[1] == mesh.shape["tensor"]
        body = in_one_kernel if fits and one_head else on_device
        return jax.shard_map(
            body, mesh=mesh, in_specs=placed, out_specs=out_placed, check_vma=False
        )(*args)

    return whole
```

```python
import functools

import jax
import jax.numpy as jnp
from jax import lax
from jax.experimental import pallas as pl
from jax.experimental.pallas import tpu as pltpu
from jax.sharding import PartitionSpec as P

D = 2048
HEAD = 128
STEPS = 2


norm_eps = 1e-06
highest = lax.Precision.HIGHEST
MESH = pl.DeviceIdType.MESH


def partner_2(block, axis, stride):
    count = lax.axis_size(axis)
    route = []
    for low in range(count):
        high = low | 1 << stride
        if high != low and high < count:
            route += [(low, high), (high, low)]
    return lax.ppermute(block, axis, route)


def rounded(values):
    return lax.optimization_barrier(values.astype(jnp.bfloat16))


def rms_scaled(values, gain_vec):
    values = values.astype(jnp.float32)
    mean_square = jnp.mean(values * values, axis=-1, keepdims=True)
    return values * lax.rsqrt(mean_square + norm_eps) * gain_vec.astype(jnp.float32)


def unit_rows(values):
    return values * lax.rsqrt(jnp.sum(values * values, axis=-1, keepdims=True) + norm_eps)


def reduce_terms(partial_value):
    term_bf = rounded(partial_value)
    return lax.psum_scatter(
        term_bf.astype(jnp.float32).astype(jnp.bfloat16), "tensor", scatter_dimension=1, tiled=True
    ).astype(jnp.float32)


def on_device(
    hidden,
    attn_gain,
    w_qkvz,
    w_ab,
    conv_weight,
    decay_log,
    dt_bias,
    norm_gain,
    w_out,
    ffn_gain,
    w_gu,
    w_down,
    state,
    conv_state,
):
    seq_count = hidden.shape[1]
    rank_here = lax.axis_index("tensor")
    half_dim = HEAD // 2
    is_odd = rank_here % 2 == 1
    carried = state
    window_state = conv_state
    outputs = []
    for step_num in range(STEPS):
        own_input = hidden[step_num]
        x_full = lax.all_gather(own_input, "tensor", axis=1, tiled=True)
        normed = rms_scaled(x_full, attn_gain).astype(jnp.bfloat16)
        projected = jnp.dot(
            normed, w_qkvz.reshape(D, -1), preferred_element_type=jnp.float32
        ).reshape(seq_count, 1, 3 * HEAD)
        gate_in = jnp.dot(normed, w_ab.reshape(D, -1), preferred_element_type=jnp.float32).reshape(
            seq_count, 1, 2
        )
        mixed = rounded(projected[:, :, : 2 * HEAD])
        window = jnp.concatenate([window_state, mixed[:, None]], axis=1)
        window_state = window[:, 1:]
        conv_sum = jnp.sum(
            window.astype(jnp.float32) * conv_weight.astype(jnp.float32)[None], axis=1
        )
        conv_bf = rounded(jax.nn.silu(conv_sum))
        own_halves = conv_bf[:, 0, :HEAD]
        partner = partner_2(own_halves, "tensor", 0)
        first_part = jnp.where(is_odd, partner, own_halves)
        second_part = jnp.where(is_odd, own_halves, partner)
        query_head = jnp.concatenate(
            [first_part[:, :half_dim], second_part[:, :half_dim]], axis=1
        ).astype(jnp.float32)
        key_head = jnp.concatenate(
            [first_part[:, half_dim:], second_part[:, half_dim:]], axis=1
        ).astype(jnp.float32)
        queries = (unit_rows(query_head) * HEAD ** (-0.5))[:, None]
        key_vecs = unit_rows(key_head)[:, None]
        value_vecs = conv_bf[:, :, HEAD:].astype(jnp.float32)
        alpha = jnp.exp(-jnp.exp(decay_log) * jax.nn.softplus(gate_in[:, :, 0] + dt_bias))
        beta = jax.nn.sigmoid(gate_in[:, :, 1])
        carried = carried * alpha[:, :, None, None]
        predicted = jnp.einsum("bhk,bhkv->bhv", key_vecs, carried, precision=highest)
        delta = (value_vecs - predicted) * beta[:, :, None]
        carried = carried + key_vecs[:, :, :, None] * delta[:, :, None, :]
        core = jnp.einsum("bhk,bhkv->bhv", queries, carried, precision=highest)
        gated = (rms_scaled(core, norm_gain) * jax.nn.silu(projected[:, :, 2 * HEAD :])).astype(
            jnp.bfloat16
        )
        partial_value = jnp.dot(
            gated.reshape(seq_count, HEAD), w_out, preferred_element_type=jnp.float32
        )
        attention = reduce_terms(partial_value)
        own_mid = rounded(own_input.astype(jnp.float32) + attention)
        middle = lax.all_gather(own_mid, "tensor", axis=1, tiled=True).astype(jnp.float32)
        middle_own = own_mid.astype(jnp.float32)
        normed_mid = rms_scaled(middle, ffn_gain).astype(jnp.bfloat16)
        gate_out = jnp.dot(normed_mid, w_gu[0], preferred_element_type=jnp.float32)
        up_out = jnp.dot(normed_mid, w_gu[1], preferred_element_type=jnp.float32)
        inner = (jax.nn.silu(gate_out) * up_out).astype(jnp.bfloat16)
        feed_partial = jnp.dot(inner, w_down, preferred_element_type=jnp.float32)
        feed_own = reduce_terms(feed_partial)
        outputs.append((middle_own + feed_own).astype(jnp.bfloat16))
    return (jnp.stack(outputs), carried, window_state)


def lane_tiles_fit(mesh, width, hidden_units):
    count = mesh.shape["tensor"]
    return count % 2 == 0 and width % (count * 128) == 0 and hidden_units % (count * 128) == 0


def sigmoid(values):
    return 1.0 / (1.0 + jnp.exp(-values))


def mixer_kernel(
    count,
    hidden,
    attn_gain,
    w_qkvz,
    w_ab,
    conv_weight,
    decay_log,
    dt_bias,
    norm_gain,
    w_out,
    ffn_gain,
    w_gu,
    w_down,
    state,
    conv_state,
    out_hidden,
    out_state,
    out_conv,
    x_all,
    qkvz,
    ab,
    taps,
    out_w,
    gu,
    down,
    carried,
    window,
    gains_in,
    head_gain,
    gains,
    split_state,
    vecs,
    products,
    decay,
    half_send,
    half_recv,
    att_send,
    att_recv,
    mid_all,
    feed_send,
    feed_recv,
    act,
    hidden_out,
    conv_out_buf,
    local_sem,
    x_sems,
    half_sems,
    att_sems,
    mid_sems,
    feed_sems,
):
    me = lax.axis_index("tensor")
    steps, seqs, width = hidden.shape
    rows = steps * seqs
    units = w_down.shape[0]
    f32, bf16 = jnp.float32, jnp.bfloat16

    def peer(index):
        pair = lax.rem(me // 2 + index // 2, count // 2)
        return 2 * pair + lax.rem(lax.rem(me, 2) + lax.rem(index, 2), 2)

    partner = peer(1)

    loads = []

    def load(src, dst):
        copy = pltpu.make_async_copy(src, dst, local_sem.at[len(loads)])
        copy.start()
        loads.append(copy)
        return copy

    load_x = [load(hidden.at[s], x_all.at[me, pl.ds(s * seqs, seqs)]) for s in range(steps)]
    load_gains = [load(attn_gain, gains_in.at[0]), load(ffn_gain, gains_in.at[1])]
    load_qkvz = [load(w_qkvz, qkvz), load(w_ab, ab)]
    load_state = load(state, carried)
    load_conv = [load(conv_weight, taps), load(conv_state, window)]
    load_norm = load(norm_gain, head_gain)
    load_out = load(w_out, out_w)
    load_gu = [load(w_gu.at[0], gu.at[0]), load(w_gu.at[1], gu.at[1])]
    load_down = load(w_down, down)

    barrier = pltpu.get_barrier_semaphore()
    for index in range(1, count):
        pl.semaphore_signal(
            barrier, inc=1, device_id={"tensor": peer(index)}, device_id_type=MESH
        )
    pl.semaphore_wait(barrier, count - 1)

    def remote(src, dst, send, recv, target):
        return pltpu.make_async_remote_copy(
            src_ref=src,
            dst_ref=dst,
            send_sem=send,
            recv_sem=recv,
            device_id={"tensor": target},
            device_id_type=MESH,
        )

    for copy in load_x:
        copy.wait()
    sends = []
    for index in reversed(range(1, count)):
        copy = remote(
            x_all.at[me], x_all.at[me], x_sems.at[0, index], x_sems.at[1, me], peer(index)
        )
        copy.start()
        sends.append(copy)

    for copy in load_gains:
        copy.wait()
    for which in range(2):
        for part in range(count):
            for tile in range(width // 128):
                row = part * (width // 128) + tile
                gains[which, part, :, tile * 128 : (tile + 1) * 128] = gains_in[
                    which, row : row + 1, :
                ].astype(f32)
    load_state.wait()

    @pl.loop(0, seqs)
    def _(seq):
        block = carried[seq]
        high = block.astype(bf16)
        split_state[seq, :HEAD] = high
        split_state[seq, HEAD:] = (block - high.astype(f32)).astype(bf16)

    for copy in load_qkvz:
        copy.wait()

    projected = jnp.zeros((rows, 3 * HEAD), f32)
    gate_in = jnp.zeros((rows, 2), f32)
    square = jnp.zeros((rows, 1), f32)
    for index in range(count):
        src = peer(index)
        if index:
            remote(
                x_all.at[src], x_all.at[src], x_sems.at[0, index], x_sems.at[1, src], src
            ).wait_recv()
        block = x_all[src].astype(f32)
        square += jnp.sum(block * block, axis=-1, keepdims=True)
        scaled = (block * gains[0, src]).astype(bf16)
        span = pl.ds(pl.multiple_of(src * width, width), width)
        projected += jnp.dot(scaled, qkvz[span, :], preferred_element_type=f32)
        gate_in += lax.dot_general(
            scaled, ab[:, span], (((1,), (1,)), ((), ())), preferred_element_type=f32
        )
    factor = lax.rsqrt(square / (count * width) + norm_eps)
    projected = projected * factor
    gate_in = gate_in * factor

    for copy in load_conv:
        copy.wait()
    mixed = projected[:, : 2 * HEAD].astype(bf16)
    kept = window.shape[0]
    for row in range(kept):
        place = row + steps - kept
        if place < 0:
            conv_out_buf[row] = window[row + steps]
        else:
            conv_out_buf[row] = mixed[place * seqs : (place + 1) * seqs]
    history = [window[row].astype(f32) for row in range(kept)]
    history += [mixed[s * seqs : (s + 1) * seqs].astype(f32) for s in range(steps)]
    tap_rows = taps[...].astype(f32)
    conv_steps = []
    for s in range(steps):
        total = history[s] * tap_rows[0:1]
        for tap in range(1, kept + 1):
            total += history[s + tap] * tap_rows[tap : tap + 1]
        conv_steps.append((total * sigmoid(total)).astype(bf16))
    conv_bf = jnp.concatenate(conv_steps, axis=0)
    half_send[...] = conv_bf[:, :HEAD]
    half_copy = remote(
        half_send, half_recv, half_sems.at[0], half_sems.at[1], partner
    )
    half_copy.start()
    store_conv = pltpu.make_async_copy(conv_out_buf, out_conv, local_sem.at[len(loads)])
    store_conv.start()

    shift = jnp.full((rows, 1), dt_bias[0], f32)
    rate = jnp.exp(jnp.full((rows, 1), decay_log[0], f32))
    biased = gate_in[:, 0:1] + shift
    softplus = jnp.maximum(biased, 0.0) + jnp.log1p(jnp.exp(-jnp.abs(biased)))
    alpha = jnp.exp(-rate * softplus)
    beta = sigmoid(gate_in[:, 1:2])
    out_gate = projected[:, 2 * HEAD :]
    out_gate = out_gate * sigmoid(out_gate)
    value_vecs = conv_bf[:, HEAD:].astype(f32)
    own = conv_bf[:, :HEAD].astype(f32)
    is_odd = lax.rem(me, 2) == 1
    low_lanes = lax.broadcasted_iota(jnp.int32, (rows, HEAD), 1) < HEAD // 2

    half_copy.wait_recv()
    other = half_recv[...].astype(f32)
    first = jnp.where(is_odd, other, own)
    second = jnp.where(is_odd, own, other)
    query_raw = jnp.where(low_lanes, first, pltpu.roll(second, HEAD // 2, 1))
    key_raw = jnp.where(low_lanes, pltpu.roll(first, HEAD // 2, 1), second)
    query_scale = lax.rsqrt(
        jnp.sum(query_raw * query_raw, axis=-1, keepdims=True) + norm_eps
    ) * HEAD ** (-0.5)
    key_scale = lax.rsqrt(jnp.sum(key_raw * key_raw, axis=-1, keepdims=True) + norm_eps)

    for s in range(steps):
        part = slice(s * seqs, (s + 1) * seqs)
        vecs[:, 2 * s, :] = key_raw[part]
        vecs[:, 2 * s + 1, :] = query_raw[part]
    for row in range(2 * steps, 8):
        vecs[:, row, :] = jnp.zeros((seqs, HEAD), f32)

    group = 8

    @pl.loop(0, seqs // group)
    def _(outer):
        for inner_seq in range(group):
            seq = outer * group + inner_seq
            lhs = vecs[seq].astype(bf16)
            products[seq] = jnp.dot(
                jnp.concatenate([lhs, lhs], axis=1),
                split_state[seq],
                preferred_element_type=f32,
            )

    queries = query_raw * query_scale
    key_vecs = key_raw * key_scale
    cut = [slice(s * seqs, (s + 1) * seqs) for s in range(steps)]
    deltas, cores = [], []
    total_decay = jnp.ones((seqs, 1), f32)
    for s in range(steps):
        a = alpha[cut[s]]
        total_decay = total_decay * a
        predicted = products[:, 2 * s, :] * (key_scale[cut[s]] * total_decay)
        read = products[:, 2 * s + 1, :] * (query_scale[cut[s]] * total_decay)
        deltas = [d * a for d in deltas]
        for t in range(s):
            predicted += deltas[t] * jnp.sum(
                key_vecs[cut[s]] * key_vecs[cut[t]], axis=-1, keepdims=True
            )
            read += deltas[t] * jnp.sum(
                queries[cut[s]] * key_vecs[cut[t]], axis=-1, keepdims=True
            )
        delta = (value_vecs[cut[s]] - predicted) * beta[cut[s]]
        read += delta * jnp.sum(queries[cut[s]] * key_vecs[cut[s]], axis=-1, keepdims=True)
        deltas.append(delta)
        cores.append(read)
    core = jnp.concatenate(cores, axis=0)
    load_norm.wait()
    core_factor = lax.rsqrt(jnp.mean(core * core, axis=-1, keepdims=True) + norm_eps)
    gated = (core * core_factor * head_gain[...].astype(f32) * out_gate).astype(bf16)

    load_out.wait()
    for index in reversed(range(count)):
        target = peer(index)
        span = pl.ds(pl.multiple_of(target * width, width), width)
        term = jnp.dot(gated, out_w[:, span], preferred_element_type=f32).astype(bf16)
        if index == 0:
            attention = term.astype(f32)
        else:
            att_send[index] = term
            copy = remote(
                att_send.at[index], att_recv.at[me], att_sems.at[0, index], att_sems.at[1, me], target
            )
            copy.start()
            sends.append(copy)

    decay[...] = jnp.broadcast_to(total_decay, (seqs, HEAD))
    for s in range(steps):
        written = deltas[s] * key_scale[cut[s]]
        high = written.astype(bf16).astype(f32)
        vecs[:, 4 * s // 2, :] = key_raw[cut[s]]
        vecs[:, 4 * s // 2 + 1, :] = key_raw[cut[s]]
        products[:, 2 * s, :] = high
        products[:, 2 * s + 1, :] = written - high
    for row in range(2 * steps, 8):
        products[:, row, :] = jnp.zeros((seqs, HEAD), f32)

    @pl.loop(0, seqs // group)
    def _(outer):
        for inner_seq in range(group):
            seq = outer * group + inner_seq
            columns = jnp.transpose(vecs[seq]).astype(bf16)
            carried[seq] = carried[seq] * decay[pl.ds(seq, 1), :] + jnp.dot(
                columns, products[seq].astype(bf16), preferred_element_type=f32
            )

    store_state = pltpu.make_async_copy(carried, out_state, local_sem.at[len(loads) + 1])
    store_state.start()

    for index in range(1, count):
        src = peer(index)
        remote(
            att_send.at[index], att_recv.at[src], att_sems.at[0, index], att_sems.at[1, src], src
        ).wait_recv()
        attention += att_recv[src].astype(f32)
    mid_own = (x_all[me].astype(f32) + attention).astype(bf16)
    mid_all[me] = mid_own
    for index in reversed(range(1, count)):
        copy = remote(
            mid_all.at[me], mid_all.at[me], mid_sems.at[0, index], mid_sems.at[1, me], peer(index)
        )
        copy.start()
        sends.append(copy)

    for copy in load_gu:
        copy.wait()
    square = jnp.zeros((rows, 1), f32)
    for index in range(count):
        src = peer(index)
        if index:
            remote(
                mid_all.at[src], mid_all.at[src], mid_sems.at[0, index], mid_sems.at[1, src], src
            ).wait_recv()
        block = mid_all[src].astype(f32)
        square += jnp.sum(block * block, axis=-1, keepdims=True)
        scaled = (block * gains[1, src]).astype(bf16)
        span = pl.ds(pl.multiple_of(src * width, width), width)
        for which in range(2):
            term = jnp.dot(scaled, gu[which, span, :], preferred_element_type=f32)
            if index == 0:
                act[which] = term
            else:
                act[which] += term
    factor = lax.rsqrt(square / (count * width) + norm_eps)
    gate_out = act[0] * factor
    inner = (gate_out * sigmoid(gate_out) * (act[1] * factor)).astype(bf16)

    load_down.wait()
    for index in reversed(range(count)):
        target = peer(index)
        span = pl.ds(pl.multiple_of(target * width, width), width)
        term = jnp.dot(inner, down[:, span], preferred_element_type=f32).astype(bf16)
        if index == 0:
            feed = term.astype(f32)
        else:
            feed_send[index] = term
            copy = remote(
                feed_send.at[index], feed_recv.at[me], feed_sems.at[0, index], feed_sems.at[1, me], target
            )
            copy.start()
            sends.append(copy)
    for index in range(1, count):
        src = peer(index)
        remote(
            feed_send.at[index], feed_recv.at[src], feed_sems.at[0, index], feed_sems.at[1, src], src
        ).wait_recv()
        feed += feed_recv[src].astype(f32)
    final = (mid_all[me].astype(f32) + feed).astype(bf16)
    for s in range(steps):
        hidden_out[s] = final[cut[s]]
    store_hidden = pltpu.make_async_copy(hidden_out, out_hidden, local_sem.at[len(loads) + 2])
    store_hidden.start()
    half_copy.wait_send()
    for copy in sends:
        copy.wait_send()
    store_conv.wait()
    store_state.wait()
    store_hidden.wait()


def finish_kernel(*refs):
    sources, targets, held, sems = refs[:3], refs[3:6], refs[6:9], refs[9]
    inward, outward = [], []
    for source, target, buffer in zip(sources, targets, held):
        cuts = 4 if source.shape[0] % 4 == 0 else 1
        size = source.shape[0] // cuts
        for cut in range(cuts):
            span, place = pl.ds(cut * size, size), len(inward)
            inward.append(
                pltpu.make_async_copy(source.at[span], buffer.at[span], sems.at[0, place])
            )
            outward.append(
                pltpu.make_async_copy(buffer.at[span], target.at[span], sems.at[1, place])
            )
    for copy in inward:
        copy.start()
    for first, second in zip(inward, outward):
        first.wait()
        second.start()
    for copy in outward:
        copy.wait()


def in_one_kernel(
    hidden,
    attn_gain,
    w_qkvz,
    w_ab,
    conv_weight,
    decay_log,
    dt_bias,
    norm_gain,
    w_out,
    ffn_gain,
    w_gu,
    w_down,
    state,
    conv_state,
):
    count = lax.axis_size("tensor")
    steps, seqs, width = hidden.shape
    rows, full, units = steps * seqs, count * width, w_down.shape[0]
    kept = conv_state.shape[1]
    f32, bf16 = jnp.float32, jnp.bfloat16
    anywhere = pl.BlockSpec(memory_space=pl.ANY)
    scalar = pl.BlockSpec(memory_space=pltpu.SMEM)
    in_hbm = pl.BlockSpec(memory_space=pltpu.HBM)
    in_specs = [in_hbm] * 5 + [scalar] * 2 + [in_hbm] * 7
    vmem = pltpu.VMEM
    pair = pltpu.SemaphoreType.DMA((2, count))
    out = pl.pallas_call(
        functools.partial(mixer_kernel, count),
        out_shape=(
            jax.ShapeDtypeStruct(hidden.shape, bf16),
            jax.ShapeDtypeStruct((seqs, HEAD, HEAD), f32),
            jax.ShapeDtypeStruct((kept, seqs, 2 * HEAD), bf16),
        ),
        in_specs=in_specs,
        out_specs=(anywhere,) * 3,
        scratch_shapes=[
            vmem((count, rows, width), bf16),
            vmem((full, 3 * HEAD), bf16),
            vmem((2, full), bf16),
            vmem((kept + 1, 2 * HEAD), bf16),
            vmem((HEAD, full), bf16),
            vmem((2, full, units), bf16),
            vmem((units, full), bf16),
            vmem((seqs, HEAD, HEAD), f32),
            vmem((kept, seqs, 2 * HEAD), bf16),
            vmem((2, full // 128, 128), bf16),
            vmem((1, HEAD), bf16),
            vmem((2, count, 1, width), f32),
            vmem((seqs, 2 * HEAD, HEAD), bf16),
            vmem((seqs, 8, HEAD), f32),
            vmem((seqs, 8, HEAD), f32),
            vmem((seqs, HEAD), f32),
            vmem((rows, HEAD), bf16),
            vmem((rows, HEAD), bf16),
            vmem((count, rows, width), bf16),
            vmem((count, rows, width), bf16),
            vmem((count, rows, width), bf16),
            vmem((count, rows, width), bf16),
            vmem((count, rows, width), bf16),
            vmem((2, rows, units), f32),
            vmem(hidden.shape, bf16),
            vmem((kept, seqs, 2 * HEAD), bf16),
            pltpu.SemaphoreType.DMA((20,)),
            pair,
            pltpu.SemaphoreType.DMA((2,)),
            pair,
            pair,
            pair,
        ],
        compiler_params=pltpu.CompilerParams(
            collective_id=0, has_side_effects=True, vmem_limit_bytes=63 * 2**20
        ),
    )(
        hidden,
        attn_gain.reshape(full // 128, 128),
        w_qkvz.reshape(full, 3 * HEAD),
        w_ab.reshape(full, 2).T,
        conv_weight.reshape(kept + 1, 2 * HEAD),
        decay_log,
        dt_bias,
        norm_gain.reshape(1, HEAD),
        w_out,
        ffn_gain.reshape(full // 128, 128),
        w_gu,
        w_down,
        state.reshape(seqs, HEAD, HEAD),
        conv_state.reshape(seqs, kept, 2 * HEAD).transpose(1, 0, 2),
    )
    next_hidden, next_state, next_conv = pl.pallas_call(
        finish_kernel,
        out_shape=tuple(jax.ShapeDtypeStruct(a.shape, a.dtype) for a in out),
        in_specs=[anywhere] * 3,
        out_specs=(anywhere,) * 3,
        scratch_shapes=[pltpu.VMEM(a.shape, a.dtype) for a in out]
        + [pltpu.SemaphoreType.DMA((2, 12))],
        compiler_params=pltpu.CompilerParams(vmem_limit_bytes=63 * 2**20),
    )(*out)
    return (
        next_hidden,
        next_state[:, None],
        next_conv.transpose(1, 0, 2)[:, :, None],
    )


def solution(mesh):
    placed = (
        P(None, ("groups", "dp"), "tensor"),
        P(),
        P(None, "tensor", None),
        P(None, "tensor", None),
        P(None, "tensor", None),
        P("tensor"),
        P("tensor"),
        P(),
        P("tensor", None),
        P(),
        P(None, None, "tensor"),
        P("tensor", None),
        P(("groups", "dp"), "tensor", None, None),
        P(("groups", "dp"), None, "tensor", None),
    )
    out_placed = (placed[0], placed[12], placed[13])

    def whole(*args):
        fits = lane_tiles_fit(mesh, args[0].shape[2], args[11].shape[0])
        one_head = args[2].shape[1] == mesh.shape["tensor"]
        body = in_one_kernel if fits and one_head else on_device
        return jax.shard_map(
            body, mesh=mesh, in_specs=placed, out_specs=out_placed, check_vma=False
        )(*args)

    return whole
```

```python
import functools

import jax
import jax.numpy as jnp
from jax import lax
from jax.experimental import pallas as pl
from jax.experimental.pallas import tpu as pltpu
from jax.sharding import PartitionSpec as P

D = 2048
HEAD = 128
STEPS = 2


norm_eps = 1e-06
highest = lax.Precision.HIGHEST
MESH = pl.DeviceIdType.MESH


def partner_2(block, axis, stride):
    count = lax.axis_size(axis)
    route = []
    for low in range(count):
        high = low | 1 << stride
        if high != low and high < count:
            route += [(low, high), (high, low)]
    return lax.ppermute(block, axis, route)


def rounded(values):
    return lax.optimization_barrier(values.astype(jnp.bfloat16))


def rms_scaled(values, gain_vec):
    values = values.astype(jnp.float32)
    mean_square = jnp.mean(values * values, axis=-1, keepdims=True)
    return values * lax.rsqrt(mean_square + norm_eps) * gain_vec.astype(jnp.float32)


def unit_rows(values):
    return values * lax.rsqrt(jnp.sum(values * values, axis=-1, keepdims=True) + norm_eps)


def reduce_terms(partial_value):
    term_bf = rounded(partial_value)
    return lax.psum_scatter(
        term_bf.astype(jnp.float32).astype(jnp.bfloat16), "tensor", scatter_dimension=1, tiled=True
    ).astype(jnp.float32)


def on_device(
    hidden,
    attn_gain,
    w_qkvz,
    w_ab,
    conv_weight,
    decay_log,
    dt_bias,
    norm_gain,
    w_out,
    ffn_gain,
    w_gu,
    w_down,
    state,
    conv_state,
):
    seq_count = hidden.shape[1]
    rank_here = lax.axis_index("tensor")
    half_dim = HEAD // 2
    is_odd = rank_here % 2 == 1
    carried = state
    window_state = conv_state
    outputs = []
    for step_num in range(STEPS):
        own_input = hidden[step_num]
        x_full = lax.all_gather(own_input, "tensor", axis=1, tiled=True)
        normed = rms_scaled(x_full, attn_gain).astype(jnp.bfloat16)
        projected = jnp.dot(
            normed, w_qkvz.reshape(D, -1), preferred_element_type=jnp.float32
        ).reshape(seq_count, 1, 3 * HEAD)
        gate_in = jnp.dot(normed, w_ab.reshape(D, -1), preferred_element_type=jnp.float32).reshape(
            seq_count, 1, 2
        )
        mixed = rounded(projected[:, :, : 2 * HEAD])
        window = jnp.concatenate([window_state, mixed[:, None]], axis=1)
        window_state = window[:, 1:]
        conv_sum = jnp.sum(
            window.astype(jnp.float32) * conv_weight.astype(jnp.float32)[None], axis=1
        )
        conv_bf = rounded(jax.nn.silu(conv_sum))
        own_halves = conv_bf[:, 0, :HEAD]
        partner = partner_2(own_halves, "tensor", 0)
        first_part = jnp.where(is_odd, partner, own_halves)
        second_part = jnp.where(is_odd, own_halves, partner)
        query_head = jnp.concatenate(
            [first_part[:, :half_dim], second_part[:, :half_dim]], axis=1
        ).astype(jnp.float32)
        key_head = jnp.concatenate(
            [first_part[:, half_dim:], second_part[:, half_dim:]], axis=1
        ).astype(jnp.float32)
        queries = (unit_rows(query_head) * HEAD ** (-0.5))[:, None]
        key_vecs = unit_rows(key_head)[:, None]
        value_vecs = conv_bf[:, :, HEAD:].astype(jnp.float32)
        alpha = jnp.exp(-jnp.exp(decay_log) * jax.nn.softplus(gate_in[:, :, 0] + dt_bias))
        beta = jax.nn.sigmoid(gate_in[:, :, 1])
        carried = carried * alpha[:, :, None, None]
        predicted = jnp.einsum("bhk,bhkv->bhv", key_vecs, carried, precision=highest)
        delta = (value_vecs - predicted) * beta[:, :, None]
        carried = carried + key_vecs[:, :, :, None] * delta[:, :, None, :]
        core = jnp.einsum("bhk,bhkv->bhv", queries, carried, precision=highest)
        gated = (rms_scaled(core, norm_gain) * jax.nn.silu(projected[:, :, 2 * HEAD :])).astype(
            jnp.bfloat16
        )
        partial_value = jnp.dot(
            gated.reshape(seq_count, HEAD), w_out, preferred_element_type=jnp.float32
        )
        attention = reduce_terms(partial_value)
        own_mid = rounded(own_input.astype(jnp.float32) + attention)
        middle = lax.all_gather(own_mid, "tensor", axis=1, tiled=True).astype(jnp.float32)
        middle_own = own_mid.astype(jnp.float32)
        normed_mid = rms_scaled(middle, ffn_gain).astype(jnp.bfloat16)
        gate_out = jnp.dot(normed_mid, w_gu[0], preferred_element_type=jnp.float32)
        up_out = jnp.dot(normed_mid, w_gu[1], preferred_element_type=jnp.float32)
        inner = (jax.nn.silu(gate_out) * up_out).astype(jnp.bfloat16)
        feed_partial = jnp.dot(inner, w_down, preferred_element_type=jnp.float32)
        feed_own = reduce_terms(feed_partial)
        outputs.append((middle_own + feed_own).astype(jnp.bfloat16))
    return (jnp.stack(outputs), carried, window_state)


def lane_tiles_fit(mesh, width, hidden_units):
    count = mesh.shape["tensor"]
    plane_count = mesh.shape["groups"] * mesh.shape["dp"]
    if HEAD % (plane_count * 16):
        return False
    return count % 2 == 0 and width % (count * 128) == 0 and hidden_units % (count * 128) == 0


def sigmoid(values):
    return 1.0 / (1.0 + jnp.exp(-values))


def mixer_kernel(
    count,
    planes,
    hidden,
    attn_gain,
    w_qkvz,
    w_ab,
    conv_weight,
    decay_log,
    dt_bias,
    norm_gain,
    w_out,
    ffn_gain,
    w_gu,
    w_down,
    state,
    conv_state,
    out_hidden,
    out_state,
    out_conv,
    x_all,
    qkvz,
    ab,
    taps,
    out_w,
    gu,
    down,
    carried,
    window,
    gains_in,
    head_gain,
    gains,
    split_state,
    vecs,
    products,
    decay,
    half_send,
    half_recv,
    gated_all,
    w_peers,
    mid_all,
    feed_send,
    feed_recv,
    act,
    hidden_out,
    conv_out_buf,
    local_sem,
    x_sems,
    half_sems,
    gated_sems,
    w_sems,
    plane_sems,
    mid_sems,
    feed_sems,
):
    me = lax.axis_index("tensor")
    steps, seqs, width = hidden.shape
    rows = steps * seqs
    units = w_down.shape[0]
    f32, bf16 = jnp.float32, jnp.bfloat16

    def peer(index):
        pair = lax.rem(me // 2 + index // 2, count // 2)
        return 2 * pair + lax.rem(lax.rem(me, 2) + lax.rem(index, 2), 2)

    partner = peer(1)
    per_group = planes[1]
    plane_count = planes[0] * planes[1]
    here = lax.axis_index("groups") * per_group + lax.axis_index("dp")
    piece = HEAD // plane_count
    own_rows = pl.ds(pl.multiple_of(here * piece, piece), piece)

    def columns_of(index):
        return pl.ds(pl.multiple_of(index * width, width), width)

    def plane_peer(offset):
        return lax.rem(here + offset, plane_count)

    def plane_id(place):
        return {"groups": place // per_group, "dp": lax.rem(place, per_group)}

    loads = []

    def load(src, dst):
        copy = pltpu.make_async_copy(src, dst, local_sem.at[len(loads)])
        copy.start()
        loads.append(copy)
        return copy

    load_x = [load(hidden.at[s], x_all.at[me, pl.ds(s * seqs, seqs)]) for s in range(steps)]
    load_gains = [load(attn_gain, gains_in.at[0]), load(ffn_gain, gains_in.at[1])]
    load_qkvz = [load(w_qkvz, qkvz), load(w_ab, ab)]
    load_state = load(state, carried)
    load_conv = [load(conv_weight, taps), load(conv_state, window)]
    load_norm = load(norm_gain, head_gain)
    load_out = load(w_out.at[:, columns_of(me)], out_w)
    load_gu = [load(w_gu.at[0], gu.at[0]), load(w_gu.at[1], gu.at[1])]
    load_down = load(w_down, down)

    barrier = pltpu.get_barrier_semaphore()
    for index in range(1, count):
        pl.semaphore_signal(
            barrier, inc=1, device_id={"tensor": peer(index)}, device_id_type=MESH
        )
    for offset in range(1, plane_count):
        pl.semaphore_signal(
            barrier, inc=1, device_id=plane_id(plane_peer(offset)), device_id_type=MESH
        )
    pl.semaphore_wait(barrier, count - 1 + plane_count - 1)

    def remote(src, dst, send, recv, target):
        return pltpu.make_async_remote_copy(
            src_ref=src,
            dst_ref=dst,
            send_sem=send,
            recv_sem=recv,
            device_id=target if isinstance(target, dict) else {"tensor": target},
            device_id_type=MESH,
        )

    for copy in load_x:
        copy.wait()
    sends = []
    for index in reversed(range(1, count)):
        copy = remote(
            x_all.at[me], x_all.at[me], x_sems.at[0, index], x_sems.at[1, me], peer(index)
        )
        copy.start()
        sends.append(copy)

    half = count // 2
    for index in range(1, count):
        slot = 2 * ((half - index // 2) % half) + index % 2 - 1
        copy = remote(
            w_out.at[own_rows, columns_of(peer(index))],
            w_peers.at[here, slot],
            w_sems.at[0, index],
            w_sems.at[1, slot + 1],
            peer(index),
        )
        copy.start()
        sends.append(copy)

    for copy in load_gains:
        copy.wait()
    for which in range(2):
        for part in range(count):
            for tile in range(width // 128):
                row = part * (width // 128) + tile
                gains[which, part, :, tile * 128 : (tile + 1) * 128] = gains_in[
                    which, row : row + 1, :
                ].astype(f32)
    load_state.wait()

    @pl.loop(0, seqs)
    def _(seq):
        block = carried[seq]
        high = block.astype(bf16)
        split_state[seq, :HEAD] = high
        split_state[seq, HEAD:] = (block - high.astype(f32)).astype(bf16)

    for copy in load_qkvz:
        copy.wait()

    projected = jnp.zeros((rows, 3 * HEAD), f32)
    gate_in = jnp.zeros((rows, 2), f32)
    square = jnp.zeros((rows, 1), f32)
    for index in range(count):
        src = peer(index)
        if index == count - 1:
            for slot in range(count - 1):
                remote(
                    w_peers.at[here, slot],
                    w_peers.at[here, slot],
                    w_sems.at[0, slot + 1],
                    w_sems.at[1, slot + 1],
                    peer(slot + 1),
                ).wait_recv()
            for offset in range(1, plane_count):
                copy = remote(
                    w_peers.at[here],
                    w_peers.at[here],
                    plane_sems.at[0, offset],
                    plane_sems.at[1, here],
                    plane_id(plane_peer(offset)),
                )
                copy.start()
                sends.append(copy)
        if index:
            remote(
                x_all.at[src], x_all.at[src], x_sems.at[0, index], x_sems.at[1, src], src
            ).wait_recv()
        block = x_all[src].astype(f32)
        square += jnp.sum(block * block, axis=-1, keepdims=True)
        scaled = (block * gains[0, src]).astype(bf16)
        span = pl.ds(pl.multiple_of(src * width, width), width)
        projected += jnp.dot(scaled, qkvz[span, :], preferred_element_type=f32)
        gate_in += lax.dot_general(
            scaled, ab[:, span], (((1,), (1,)), ((), ())), preferred_element_type=f32
        )
    factor = lax.rsqrt(square / (count * width) + norm_eps)
    projected = projected * factor
    gate_in = gate_in * factor

    for copy in load_conv:
        copy.wait()
    mixed = projected[:, : 2 * HEAD].astype(bf16)
    kept = window.shape[0]
    for row in range(kept):
        place = row + steps - kept
        if place < 0:
            conv_out_buf[row] = window[row + steps]
        else:
            conv_out_buf[row] = mixed[place * seqs : (place + 1) * seqs]
    history = [window[row].astype(f32) for row in range(kept)]
    history += [mixed[s * seqs : (s + 1) * seqs].astype(f32) for s in range(steps)]
    tap_rows = taps[...].astype(f32)
    conv_steps = []
    for s in range(steps):
        total = history[s] * tap_rows[0:1]
        for tap in range(1, kept + 1):
            total += history[s + tap] * tap_rows[tap : tap + 1]
        conv_steps.append((total * sigmoid(total)).astype(bf16))
    conv_bf = jnp.concatenate(conv_steps, axis=0)
    half_send[...] = conv_bf[:, :HEAD]
    half_copy = remote(
        half_send, half_recv, half_sems.at[0], half_sems.at[1], partner
    )
    half_copy.start()
    store_conv = pltpu.make_async_copy(conv_out_buf, out_conv, local_sem.at[len(loads)])
    store_conv.start()

    shift = jnp.full((rows, 1), dt_bias[0], f32)
    rate = jnp.exp(jnp.full((rows, 1), decay_log[0], f32))
    biased = gate_in[:, 0:1] + shift
    softplus = jnp.maximum(biased, 0.0) + jnp.log1p(jnp.exp(-jnp.abs(biased)))
    alpha = jnp.exp(-rate * softplus)
    beta = sigmoid(gate_in[:, 1:2])
    out_gate = projected[:, 2 * HEAD :]
    out_gate = out_gate * sigmoid(out_gate)
    value_vecs = conv_bf[:, HEAD:].astype(f32)
    own = conv_bf[:, :HEAD].astype(f32)
    is_odd = lax.rem(me, 2) == 1
    low_lanes = lax.broadcasted_iota(jnp.int32, (rows, HEAD), 1) < HEAD // 2

    half_copy.wait_recv()
    other = half_recv[...].astype(f32)
    first = jnp.where(is_odd, other, own)
    second = jnp.where(is_odd, own, other)
    query_raw = jnp.where(low_lanes, first, pltpu.roll(second, HEAD // 2, 1))
    key_raw = jnp.where(low_lanes, pltpu.roll(first, HEAD // 2, 1), second)
    query_scale = lax.rsqrt(
        jnp.sum(query_raw * query_raw, axis=-1, keepdims=True) + norm_eps
    ) * HEAD ** (-0.5)
    key_scale = lax.rsqrt(jnp.sum(key_raw * key_raw, axis=-1, keepdims=True) + norm_eps)

    for s in range(steps):
        part = slice(s * seqs, (s + 1) * seqs)
        vecs[:, 2 * s, :] = key_raw[part]
        vecs[:, 2 * s + 1, :] = query_raw[part]
    for row in range(2 * steps, 8):
        vecs[:, row, :] = jnp.zeros((seqs, HEAD), f32)

    group = 8

    @pl.loop(0, seqs // group)
    def _(outer):
        for inner_seq in range(group):
            seq = outer * group + inner_seq
            lhs = vecs[seq].astype(bf16)
            products[seq] = jnp.dot(
                jnp.concatenate([lhs, lhs], axis=1),
                split_state[seq],
                preferred_element_type=f32,
            )

    queries = query_raw * query_scale
    key_vecs = key_raw * key_scale
    cut = [slice(s * seqs, (s + 1) * seqs) for s in range(steps)]
    deltas, cores = [], []
    total_decay = jnp.ones((seqs, 1), f32)
    for s in range(steps):
        a = alpha[cut[s]]
        total_decay = total_decay * a
        predicted = products[:, 2 * s, :] * (key_scale[cut[s]] * total_decay)
        read = products[:, 2 * s + 1, :] * (query_scale[cut[s]] * total_decay)
        deltas = [d * a for d in deltas]
        for t in range(s):
            predicted += deltas[t] * jnp.sum(
                key_vecs[cut[s]] * key_vecs[cut[t]], axis=-1, keepdims=True
            )
            read += deltas[t] * jnp.sum(
                queries[cut[s]] * key_vecs[cut[t]], axis=-1, keepdims=True
            )
        delta = (value_vecs[cut[s]] - predicted) * beta[cut[s]]
        read += delta * jnp.sum(queries[cut[s]] * key_vecs[cut[s]], axis=-1, keepdims=True)
        deltas.append(delta)
        cores.append(read)
    core = jnp.concatenate(cores, axis=0)
    load_norm.wait()
    core_factor = lax.rsqrt(jnp.mean(core * core, axis=-1, keepdims=True) + norm_eps)
    gated = (core * core_factor * head_gain[...].astype(f32) * out_gate).astype(bf16)

    gated_all[me] = gated
    for index in reversed(range(1, count)):
        copy = remote(
            gated_all.at[me], gated_all.at[me], gated_sems.at[0, index], gated_sems.at[1, me], peer(index)
        )
        copy.start()
        sends.append(copy)

    decay[...] = jnp.broadcast_to(total_decay, (seqs, HEAD))
    for s in range(steps):
        written = deltas[s] * key_scale[cut[s]]
        high = written.astype(bf16).astype(f32)
        vecs[:, 4 * s // 2, :] = key_raw[cut[s]]
        vecs[:, 4 * s // 2 + 1, :] = key_raw[cut[s]]
        products[:, 2 * s, :] = high
        products[:, 2 * s + 1, :] = written - high
    for row in range(2 * steps, 8):
        products[:, row, :] = jnp.zeros((seqs, HEAD), f32)

    @pl.loop(0, seqs // group)
    def _(outer):
        for inner_seq in range(group):
            seq = outer * group + inner_seq
            columns = jnp.transpose(vecs[seq]).astype(bf16)
            carried[seq] = carried[seq] * decay[pl.ds(seq, 1), :] + jnp.dot(
                columns, products[seq].astype(bf16), preferred_element_type=f32
            )

    store_state = pltpu.make_async_copy(carried, out_state, local_sem.at[len(loads) + 1])
    store_state.start()

    load_out.wait()
    attention = jnp.dot(gated, out_w[...], preferred_element_type=f32).astype(bf16).astype(f32)
    for offset in range(1, plane_count):
        place = plane_peer(offset)
        remote(
            w_peers.at[place],
            w_peers.at[place],
            plane_sems.at[0, offset],
            plane_sems.at[1, place],
            plane_id(place),
        ).wait_recv()
    for index in range(1, count):
        src = peer(index)
        remote(
            gated_all.at[src], gated_all.at[src], gated_sems.at[0, index], gated_sems.at[1, src], src
        ).wait_recv()
        weight = w_peers[:, index - 1].reshape(HEAD, width)
        term = jnp.dot(gated_all[src], weight, preferred_element_type=f32)
        attention += term.astype(bf16).astype(f32)
    mid_own = (x_all[me].astype(f32) + attention).astype(bf16)
    mid_all[me] = mid_own
    for index in reversed(range(1, count)):
        copy = remote(
            mid_all.at[me], mid_all.at[me], mid_sems.at[0, index], mid_sems.at[1, me], peer(index)
        )
        copy.start()
        sends.append(copy)

    for copy in load_gu:
        copy.wait()
    square = jnp.zeros((rows, 1), f32)
    for index in range(count):
        src = peer(index)
        if index:
            remote(
                mid_all.at[src], mid_all.at[src], mid_sems.at[0, index], mid_sems.at[1, src], src
            ).wait_recv()
        block = mid_all[src].astype(f32)
        square += jnp.sum(block * block, axis=-1, keepdims=True)
        scaled = (block * gains[1, src]).astype(bf16)
        span = pl.ds(pl.multiple_of(src * width, width), width)
        for which in range(2):
            term = jnp.dot(scaled, gu[which, span, :], preferred_element_type=f32)
            if index == 0:
                act[which] = term
            else:
                act[which] += term
    factor = lax.rsqrt(square / (count * width) + norm_eps)
    gate_out = act[0] * factor
    inner = (gate_out * sigmoid(gate_out) * (act[1] * factor)).astype(bf16)

    load_down.wait()
    for index in reversed(range(count)):
        target = peer(index)
        span = pl.ds(pl.multiple_of(target * width, width), width)
        term = jnp.dot(inner, down[:, span], preferred_element_type=f32).astype(bf16)
        if index == 0:
            feed = term.astype(f32)
        else:
            feed_send[index] = term
            copy = remote(
                feed_send.at[index], feed_recv.at[me], feed_sems.at[0, index], feed_sems.at[1, me], target
            )
            copy.start()
            sends.append(copy)
    for index in range(1, count):
        src = peer(index)
        remote(
            feed_send.at[index], feed_recv.at[src], feed_sems.at[0, index], feed_sems.at[1, src], src
        ).wait_recv()
        feed += feed_recv[src].astype(f32)
    final = (mid_all[me].astype(f32) + feed).astype(bf16)
    for s in range(steps):
        hidden_out[s] = final[cut[s]]
    store_hidden = pltpu.make_async_copy(hidden_out, out_hidden, local_sem.at[len(loads) + 2])
    store_hidden.start()
    half_copy.wait_send()
    for copy in sends:
        copy.wait_send()
    store_conv.wait()
    store_state.wait()
    store_hidden.wait()


def finish_kernel(*refs):
    sources, targets, held, sems = refs[:3], refs[3:6], refs[6:9], refs[9]
    inward, outward = [], []
    for source, target, buffer in zip(sources, targets, held):
        cuts = 4 if source.shape[0] % 4 == 0 else 1
        size = source.shape[0] // cuts
        for cut in range(cuts):
            span, place = pl.ds(cut * size, size), len(inward)
            inward.append(
                pltpu.make_async_copy(source.at[span], buffer.at[span], sems.at[0, place])
            )
            outward.append(
                pltpu.make_async_copy(buffer.at[span], target.at[span], sems.at[1, place])
            )
    for copy in inward:
        copy.start()
    for first, second in zip(inward, outward):
        first.wait()
        second.start()
    for copy in outward:
        copy.wait()


def in_one_kernel(
    hidden,
    attn_gain,
    w_qkvz,
    w_ab,
    conv_weight,
    decay_log,
    dt_bias,
    norm_gain,
    w_out,
    ffn_gain,
    w_gu,
    w_down,
    state,
    conv_state,
):
    count = lax.axis_size("tensor")
    steps, seqs, width = hidden.shape
    rows, full, units = steps * seqs, count * width, w_down.shape[0]
    kept = conv_state.shape[1]
    planes = (lax.axis_size("groups"), lax.axis_size("dp"))
    plane_count = planes[0] * planes[1]
    f32, bf16 = jnp.float32, jnp.bfloat16
    anywhere = pl.BlockSpec(memory_space=pl.ANY)
    scalar = pl.BlockSpec(memory_space=pltpu.SMEM)
    in_hbm = pl.BlockSpec(memory_space=pltpu.HBM)
    in_specs = [in_hbm] * 5 + [scalar] * 2 + [in_hbm] * 7
    vmem = pltpu.VMEM
    pair = pltpu.SemaphoreType.DMA((2, count))
    out = pl.pallas_call(
        functools.partial(mixer_kernel, count, planes),
        out_shape=(
            jax.ShapeDtypeStruct(hidden.shape, bf16),
            jax.ShapeDtypeStruct((seqs, HEAD, HEAD), f32),
            jax.ShapeDtypeStruct((kept, seqs, 2 * HEAD), bf16),
        ),
        in_specs=in_specs,
        out_specs=(anywhere,) * 3,
        scratch_shapes=[
            vmem((count, rows, width), bf16),
            vmem((full, 3 * HEAD), bf16),
            vmem((2, full), bf16),
            vmem((kept + 1, 2 * HEAD), bf16),
            vmem((HEAD, width), bf16),
            vmem((2, full, units), bf16),
            vmem((units, full), bf16),
            vmem((seqs, HEAD, HEAD), f32),
            vmem((kept, seqs, 2 * HEAD), bf16),
            vmem((2, full // 128, 128), bf16),
            vmem((1, HEAD), bf16),
            vmem((2, count, 1, width), f32),
            vmem((seqs, 2 * HEAD, HEAD), bf16),
            vmem((seqs, 8, HEAD), f32),
            vmem((seqs, 8, HEAD), f32),
            vmem((seqs, HEAD), f32),
            vmem((rows, HEAD), bf16),
            vmem((rows, HEAD), bf16),
            vmem((count, rows, HEAD), bf16),
            vmem((plane_count, count - 1, HEAD // plane_count, width), bf16),
            vmem((count, rows, width), bf16),
            vmem((count, rows, width), bf16),
            vmem((count, rows, width), bf16),
            vmem((2, rows, units), f32),
            vmem(hidden.shape, bf16),
            vmem((kept, seqs, 2 * HEAD), bf16),
            pltpu.SemaphoreType.DMA((20,)),
            pair,
            pltpu.SemaphoreType.DMA((2,)),
            pair,
            pair,
            pltpu.SemaphoreType.DMA((2, plane_count)),
            pair,
            pair,
        ],
        compiler_params=pltpu.CompilerParams(
            collective_id=0, has_side_effects=True, vmem_limit_bytes=63 * 2**20
        ),
    )(
        hidden,
        attn_gain.reshape(full // 128, 128),
        w_qkvz.reshape(full, 3 * HEAD),
        w_ab.reshape(full, 2).T,
        conv_weight.reshape(kept + 1, 2 * HEAD),
        decay_log,
        dt_bias,
        norm_gain.reshape(1, HEAD),
        w_out,
        ffn_gain.reshape(full // 128, 128),
        w_gu,
        w_down,
        state.reshape(seqs, HEAD, HEAD),
        conv_state.reshape(seqs, kept, 2 * HEAD).transpose(1, 0, 2),
    )
    next_hidden, next_state, next_conv = pl.pallas_call(
        finish_kernel,
        out_shape=tuple(jax.ShapeDtypeStruct(a.shape, a.dtype) for a in out),
        in_specs=[anywhere] * 3,
        out_specs=(anywhere,) * 3,
        scratch_shapes=[pltpu.VMEM(a.shape, a.dtype) for a in out]
        + [pltpu.SemaphoreType.DMA((2, 12))],
        compiler_params=pltpu.CompilerParams(vmem_limit_bytes=63 * 2**20),
    )(*out)
    return (
        next_hidden,
        next_state[:, None],
        next_conv.transpose(1, 0, 2)[:, :, None],
    )


def solution(mesh):
    placed = (
        P(None, ("groups", "dp"), "tensor"),
        P(),
        P(None, "tensor", None),
        P(None, "tensor", None),
        P(None, "tensor", None),
        P("tensor"),
        P("tensor"),
        P(),
        P("tensor", None),
        P(),
        P(None, None, "tensor"),
        P("tensor", None),
        P(("groups", "dp"), "tensor", None, None),
        P(("groups", "dp"), None, "tensor", None),
    )
    out_placed = (placed[0], placed[12], placed[13])

    def whole(*args):
        fits = lane_tiles_fit(mesh, args[0].shape[2], args[11].shape[0])
        one_head = args[2].shape[1] == mesh.shape["tensor"]
        body = in_one_kernel if fits and one_head else on_device
        return jax.shard_map(
            body, mesh=mesh, in_specs=placed, out_specs=out_placed, check_vma=False
        )(*args)

    return whole
```

```python
import functools

import jax
import jax.numpy as jnp
from jax import lax
from jax.experimental import pallas as pl
from jax.experimental.pallas import tpu as pltpu
from jax.sharding import PartitionSpec as P

D = 2048
HEAD = 128
STEPS = 2


norm_eps = 1e-06
highest = lax.Precision.HIGHEST
MESH = pl.DeviceIdType.MESH


def partner_2(block, axis, stride):
    count = lax.axis_size(axis)
    route = []
    for low in range(count):
        high = low | 1 << stride
        if high != low and high < count:
            route += [(low, high), (high, low)]
    return lax.ppermute(block, axis, route)


def rounded(values):
    return lax.optimization_barrier(values.astype(jnp.bfloat16))


def rms_scaled(values, gain_vec):
    values = values.astype(jnp.float32)
    mean_square = jnp.mean(values * values, axis=-1, keepdims=True)
    return values * lax.rsqrt(mean_square + norm_eps) * gain_vec.astype(jnp.float32)


def unit_rows(values):
    return values * lax.rsqrt(jnp.sum(values * values, axis=-1, keepdims=True) + norm_eps)


def reduce_terms(partial_value):
    term_bf = rounded(partial_value)
    return lax.psum_scatter(
        term_bf.astype(jnp.float32).astype(jnp.bfloat16), "tensor", scatter_dimension=1, tiled=True
    ).astype(jnp.float32)


def on_device(
    hidden,
    attn_gain,
    w_qkvz,
    w_ab,
    conv_weight,
    decay_log,
    dt_bias,
    norm_gain,
    w_out,
    ffn_gain,
    w_gu,
    w_down,
    state,
    conv_state,
):
    seq_count = hidden.shape[1]
    rank_here = lax.axis_index("tensor")
    half_dim = HEAD // 2
    is_odd = rank_here % 2 == 1
    carried = state
    window_state = conv_state
    outputs = []
    for step_num in range(STEPS):
        own_input = hidden[step_num]
        x_full = lax.all_gather(own_input, "tensor", axis=1, tiled=True)
        normed = rms_scaled(x_full, attn_gain).astype(jnp.bfloat16)
        projected = jnp.dot(
            normed, w_qkvz.reshape(D, -1), preferred_element_type=jnp.float32
        ).reshape(seq_count, 1, 3 * HEAD)
        gate_in = jnp.dot(normed, w_ab.reshape(D, -1), preferred_element_type=jnp.float32).reshape(
            seq_count, 1, 2
        )
        mixed = rounded(projected[:, :, : 2 * HEAD])
        window = jnp.concatenate([window_state, mixed[:, None]], axis=1)
        window_state = window[:, 1:]
        conv_sum = jnp.sum(
            window.astype(jnp.float32) * conv_weight.astype(jnp.float32)[None], axis=1
        )
        conv_bf = rounded(jax.nn.silu(conv_sum))
        own_halves = conv_bf[:, 0, :HEAD]
        partner = partner_2(own_halves, "tensor", 0)
        first_part = jnp.where(is_odd, partner, own_halves)
        second_part = jnp.where(is_odd, own_halves, partner)
        query_head = jnp.concatenate(
            [first_part[:, :half_dim], second_part[:, :half_dim]], axis=1
        ).astype(jnp.float32)
        key_head = jnp.concatenate(
            [first_part[:, half_dim:], second_part[:, half_dim:]], axis=1
        ).astype(jnp.float32)
        queries = (unit_rows(query_head) * HEAD ** (-0.5))[:, None]
        key_vecs = unit_rows(key_head)[:, None]
        value_vecs = conv_bf[:, :, HEAD:].astype(jnp.float32)
        alpha = jnp.exp(-jnp.exp(decay_log) * jax.nn.softplus(gate_in[:, :, 0] + dt_bias))
        beta = jax.nn.sigmoid(gate_in[:, :, 1])
        carried = carried * alpha[:, :, None, None]
        predicted = jnp.einsum("bhk,bhkv->bhv", key_vecs, carried, precision=highest)
        delta = (value_vecs - predicted) * beta[:, :, None]
        carried = carried + key_vecs[:, :, :, None] * delta[:, :, None, :]
        core = jnp.einsum("bhk,bhkv->bhv", queries, carried, precision=highest)
        gated = (rms_scaled(core, norm_gain) * jax.nn.silu(projected[:, :, 2 * HEAD :])).astype(
            jnp.bfloat16
        )
        partial_value = jnp.dot(
            gated.reshape(seq_count, HEAD), w_out, preferred_element_type=jnp.float32
        )
        attention = reduce_terms(partial_value)
        own_mid = rounded(own_input.astype(jnp.float32) + attention)
        middle = lax.all_gather(own_mid, "tensor", axis=1, tiled=True).astype(jnp.float32)
        middle_own = own_mid.astype(jnp.float32)
        normed_mid = rms_scaled(middle, ffn_gain).astype(jnp.bfloat16)
        gate_out = jnp.dot(normed_mid, w_gu[0], preferred_element_type=jnp.float32)
        up_out = jnp.dot(normed_mid, w_gu[1], preferred_element_type=jnp.float32)
        inner = (jax.nn.silu(gate_out) * up_out).astype(jnp.bfloat16)
        feed_partial = jnp.dot(inner, w_down, preferred_element_type=jnp.float32)
        feed_own = reduce_terms(feed_partial)
        outputs.append((middle_own + feed_own).astype(jnp.bfloat16))
    return (jnp.stack(outputs), carried, window_state)


def lane_tiles_fit(mesh, width, hidden_units):
    count = mesh.shape["tensor"]
    plane_count = mesh.shape["groups"] * mesh.shape["dp"]
    if HEAD % (plane_count * 16):
        return False
    return count % 2 == 0 and width % (count * 128) == 0 and hidden_units % (count * 128) == 0


def sigmoid(values):
    return 1.0 / (1.0 + jnp.exp(-values))


def mixer_kernel(
    count,
    planes,
    hidden,
    attn_gain,
    w_qkvz,
    w_ab,
    conv_weight,
    decay_log,
    dt_bias,
    norm_gain,
    w_out,
    ffn_gain,
    w_gu,
    w_down,
    state,
    conv_state,
    out_hidden,
    out_state,
    out_conv,
    x_all,
    qkvz,
    ab,
    taps,
    out_w,
    gu,
    down,
    carried,
    window,
    gains_in,
    head_gain,
    gains,
    split_state,
    vecs,
    products,
    decay,
    half_send,
    half_recv,
    gated_all,
    w_peers,
    mid_all,
    feed_send,
    feed_recv,
    act,
    hidden_out,
    conv_out_buf,
    local_sem,
    x_sems,
    half_sems,
    gated_sems,
    w_sems,
    plane_sems,
    mid_sems,
    feed_sems,
):
    me = lax.axis_index("tensor")
    steps, seqs, width = hidden.shape
    rows = steps * seqs
    units = w_down.shape[0]
    f32, bf16 = jnp.float32, jnp.bfloat16

    def peer(index):
        pair = lax.rem(me // 2 + index // 2, count // 2)
        return 2 * pair + lax.rem(lax.rem(me, 2) + lax.rem(index, 2), 2)

    partner = peer(1)
    per_group = planes[1]
    plane_count = planes[0] * planes[1]
    here = lax.axis_index("groups") * per_group + lax.axis_index("dp")
    piece = HEAD // plane_count
    own_rows = pl.ds(pl.multiple_of(here * piece, piece), piece)

    def columns_of(index):
        return pl.ds(pl.multiple_of(index * width, width), width)

    def plane_peer(offset):
        return lax.rem(here + offset, plane_count)

    def plane_id(place):
        return {"groups": place // per_group, "dp": lax.rem(place, per_group)}

    loads = []

    def load(src, dst):
        copy = pltpu.make_async_copy(src, dst, local_sem.at[len(loads)])
        copy.start()
        loads.append(copy)
        return copy

    load_x = [load(hidden.at[s], x_all.at[me, pl.ds(s * seqs, seqs)]) for s in range(steps)]
    load_gains = [load(attn_gain, gains_in.at[0]), load(ffn_gain, gains_in.at[1])]
    load_qkvz = [load(w_qkvz, qkvz), load(w_ab, ab)]
    load_state = load(state, carried)
    load_conv = [load(conv_weight, taps), load(conv_state, window)]
    load_norm = load(norm_gain, head_gain)
    load_out = load(w_out.at[:, columns_of(me)], out_w)
    load_gu = [load(w_gu.at[0], gu.at[0]), load(w_gu.at[1], gu.at[1])]
    load_down = load(w_down, down)

    barrier = pltpu.get_barrier_semaphore()
    for index in range(1, count):
        pl.semaphore_signal(
            barrier, inc=1, device_id={"tensor": peer(index)}, device_id_type=MESH
        )
    for offset in range(1, plane_count):
        pl.semaphore_signal(
            barrier, inc=1, device_id=plane_id(plane_peer(offset)), device_id_type=MESH
        )
    pl.semaphore_wait(barrier, count - 1 + plane_count - 1)

    def remote(src, dst, send, recv, target):
        return pltpu.make_async_remote_copy(
            src_ref=src,
            dst_ref=dst,
            send_sem=send,
            recv_sem=recv,
            device_id=target if isinstance(target, dict) else {"tensor": target},
            device_id_type=MESH,
        )

    for copy in load_x:
        copy.wait()
    sends = []
    for index in range(1, count):
        copy = remote(
            x_all.at[me], x_all.at[me], x_sems.at[0, index], x_sems.at[1, me], peer(index)
        )
        copy.start()
        sends.append(copy)

    half = count // 2
    for index in range(1, count):
        slot = 2 * ((half - index // 2) % half) + index % 2 - 1
        copy = remote(
            w_out.at[own_rows, columns_of(peer(index))],
            w_peers.at[here, slot],
            w_sems.at[0, index],
            w_sems.at[1, slot + 1],
            peer(index),
        )
        copy.start()
        sends.append(copy)

    for copy in load_gains:
        copy.wait()
    for which in range(2):
        for part in range(count):
            for tile in range(width // 128):
                row = part * (width // 128) + tile
                gains[which, part, :, tile * 128 : (tile + 1) * 128] = gains_in[
                    which, row : row + 1, :
                ].astype(f32)
    load_state.wait()

    @pl.loop(0, seqs)
    def _(seq):
        block = carried[seq]
        high = block.astype(bf16)
        split_state[seq, :HEAD] = high
        split_state[seq, HEAD:] = (block - high.astype(f32)).astype(bf16)

    for copy in load_qkvz:
        copy.wait()

    projected = jnp.zeros((rows, 3 * HEAD), f32)
    gate_in = jnp.zeros((rows, 2), f32)
    square = jnp.zeros((rows, 1), f32)
    for index in range(count):
        src = peer(index)
        if index == count - 1:
            for slot in range(count - 1):
                remote(
                    w_peers.at[here, slot],
                    w_peers.at[here, slot],
                    w_sems.at[0, slot + 1],
                    w_sems.at[1, slot + 1],
                    peer(slot + 1),
                ).wait_recv()
            for offset in range(1, plane_count):
                copy = remote(
                    w_peers.at[here],
                    w_peers.at[here],
                    plane_sems.at[0, offset],
                    plane_sems.at[1, here],
                    plane_id(plane_peer(offset)),
                )
                copy.start()
                sends.append(copy)
        if index:
            remote(
                x_all.at[src], x_all.at[src], x_sems.at[0, index], x_sems.at[1, src], src
            ).wait_recv()
        block = x_all[src].astype(f32)
        square += jnp.sum(block * block, axis=-1, keepdims=True)
        scaled = (block * gains[0, src]).astype(bf16)
        span = pl.ds(pl.multiple_of(src * width, width), width)
        projected += jnp.dot(scaled, qkvz[span, :], preferred_element_type=f32)
        gate_in += lax.dot_general(
            scaled, ab[:, span], (((1,), (1,)), ((), ())), preferred_element_type=f32
        )
    factor = lax.rsqrt(square / (count * width) + norm_eps)
    projected = projected * factor
    gate_in = gate_in * factor

    for copy in load_conv:
        copy.wait()
    mixed = projected[:, : 2 * HEAD].astype(bf16)
    kept = window.shape[0]
    for row in range(kept):
        place = row + steps - kept
        if place < 0:
            conv_out_buf[row] = window[row + steps]
        else:
            conv_out_buf[row] = mixed[place * seqs : (place + 1) * seqs]
    history = [window[row].astype(f32) for row in range(kept)]
    history += [mixed[s * seqs : (s + 1) * seqs].astype(f32) for s in range(steps)]
    tap_rows = taps[...].astype(f32)
    conv_steps = []
    for s in range(steps):
        total = history[s] * tap_rows[0:1]
        for tap in range(1, kept + 1):
            total += history[s + tap] * tap_rows[tap : tap + 1]
        conv_steps.append((total * sigmoid(total)).astype(bf16))
    conv_bf = jnp.concatenate(conv_steps, axis=0)
    half_send[...] = conv_bf[:, :HEAD]
    half_copy = remote(
        half_send, half_recv, half_sems.at[0], half_sems.at[1], partner
    )
    half_copy.start()
    store_conv = pltpu.make_async_copy(conv_out_buf, out_conv, local_sem.at[len(loads)])
    store_conv.start()

    shift = jnp.full((rows, 1), dt_bias[0], f32)
    rate = jnp.exp(jnp.full((rows, 1), decay_log[0], f32))
    biased = gate_in[:, 0:1] + shift
    softplus = jnp.maximum(biased, 0.0) + jnp.log1p(jnp.exp(-jnp.abs(biased)))
    alpha = jnp.exp(-rate * softplus)
    beta = sigmoid(gate_in[:, 1:2])
    out_gate = projected[:, 2 * HEAD :]
    out_gate = out_gate * sigmoid(out_gate)
    value_vecs = conv_bf[:, HEAD:].astype(f32)
    own = conv_bf[:, :HEAD].astype(f32)
    is_odd = lax.rem(me, 2) == 1
    low_lanes = lax.broadcasted_iota(jnp.int32, (rows, HEAD), 1) < HEAD // 2

    half_copy.wait_recv()
    other = half_recv[...].astype(f32)
    first = jnp.where(is_odd, other, own)
    second = jnp.where(is_odd, own, other)
    query_raw = jnp.where(low_lanes, first, pltpu.roll(second, HEAD // 2, 1))
    key_raw = jnp.where(low_lanes, pltpu.roll(first, HEAD // 2, 1), second)
    query_scale = lax.rsqrt(
        jnp.sum(query_raw * query_raw, axis=-1, keepdims=True) + norm_eps
    ) * HEAD ** (-0.5)
    key_scale = lax.rsqrt(jnp.sum(key_raw * key_raw, axis=-1, keepdims=True) + norm_eps)

    for s in range(steps):
        part = slice(s * seqs, (s + 1) * seqs)
        vecs[:, 2 * s, :] = key_raw[part]
        vecs[:, 2 * s + 1, :] = query_raw[part]
    for row in range(2 * steps, 8):
        vecs[:, row, :] = jnp.zeros((seqs, HEAD), f32)

    group = 8

    @pl.loop(0, seqs // group)
    def _(outer):
        for inner_seq in range(group):
            seq = outer * group + inner_seq
            lhs = vecs[seq].astype(bf16)
            products[seq] = jnp.dot(
                jnp.concatenate([lhs, lhs], axis=1),
                split_state[seq],
                preferred_element_type=f32,
            )

    queries = query_raw * query_scale
    key_vecs = key_raw * key_scale
    cut = [slice(s * seqs, (s + 1) * seqs) for s in range(steps)]
    deltas, cores = [], []
    total_decay = jnp.ones((seqs, 1), f32)
    for s in range(steps):
        a = alpha[cut[s]]
        total_decay = total_decay * a
        predicted = products[:, 2 * s, :] * (key_scale[cut[s]] * total_decay)
        read = products[:, 2 * s + 1, :] * (query_scale[cut[s]] * total_decay)
        deltas = [d * a for d in deltas]
        for t in range(s):
            predicted += deltas[t] * jnp.sum(
                key_vecs[cut[s]] * key_vecs[cut[t]], axis=-1, keepdims=True
            )
            read += deltas[t] * jnp.sum(
                queries[cut[s]] * key_vecs[cut[t]], axis=-1, keepdims=True
            )
        delta = (value_vecs[cut[s]] - predicted) * beta[cut[s]]
        read += delta * jnp.sum(queries[cut[s]] * key_vecs[cut[s]], axis=-1, keepdims=True)
        deltas.append(delta)
        cores.append(read)
    core = jnp.concatenate(cores, axis=0)
    load_norm.wait()
    core_factor = lax.rsqrt(jnp.mean(core * core, axis=-1, keepdims=True) + norm_eps)
    gated = (core * core_factor * head_gain[...].astype(f32) * out_gate).astype(bf16)

    gated_all[me] = gated
    for index in range(1, count):
        copy = remote(
            gated_all.at[me], gated_all.at[me], gated_sems.at[0, index], gated_sems.at[1, me], peer(index)
        )
        copy.start()
        sends.append(copy)

    decay[...] = jnp.broadcast_to(total_decay, (seqs, HEAD))
    for s in range(steps):
        written = deltas[s] * key_scale[cut[s]]
        high = written.astype(bf16).astype(f32)
        vecs[:, 4 * s // 2, :] = key_raw[cut[s]]
        vecs[:, 4 * s // 2 + 1, :] = key_raw[cut[s]]
        products[:, 2 * s, :] = high
        products[:, 2 * s + 1, :] = written - high
    for row in range(2 * steps, 8):
        products[:, row, :] = jnp.zeros((seqs, HEAD), f32)

    @pl.loop(0, seqs // group)
    def _(outer):
        for inner_seq in range(group):
            seq = outer * group + inner_seq
            columns = jnp.transpose(vecs[seq]).astype(bf16)
            carried[seq] = carried[seq] * decay[pl.ds(seq, 1), :] + jnp.dot(
                columns, products[seq].astype(bf16), preferred_element_type=f32
            )

    store_state = pltpu.make_async_copy(carried, out_state, local_sem.at[len(loads) + 1])
    store_state.start()

    load_out.wait()
    attention = jnp.dot(gated, out_w[...], preferred_element_type=f32).astype(bf16).astype(f32)
    for offset in range(1, plane_count):
        place = plane_peer(offset)
        remote(
            w_peers.at[place],
            w_peers.at[place],
            plane_sems.at[0, offset],
            plane_sems.at[1, place],
            plane_id(place),
        ).wait_recv()
    for index in range(1, count):
        src = peer(index)
        remote(
            gated_all.at[src], gated_all.at[src], gated_sems.at[0, index], gated_sems.at[1, src], src
        ).wait_recv()
        weight = w_peers[:, index - 1].reshape(HEAD, width)
        term = jnp.dot(gated_all[src], weight, preferred_element_type=f32)
        attention += term.astype(bf16).astype(f32)
    mid_own = (x_all[me].astype(f32) + attention).astype(bf16)
    mid_all[me] = mid_own
    for index in range(1, count):
        copy = remote(
            mid_all.at[me], mid_all.at[me], mid_sems.at[0, index], mid_sems.at[1, me], peer(index)
        )
        copy.start()
        sends.append(copy)

    for copy in load_gu:
        copy.wait()
    square = jnp.zeros((rows, 1), f32)
    for index in range(count):
        src = peer(index)
        if index:
            remote(
                mid_all.at[src], mid_all.at[src], mid_sems.at[0, index], mid_sems.at[1, src], src
            ).wait_recv()
        block = mid_all[src].astype(f32)
        square += jnp.sum(block * block, axis=-1, keepdims=True)
        scaled = (block * gains[1, src]).astype(bf16)
        span = pl.ds(pl.multiple_of(src * width, width), width)
        for which in range(2):
            term = jnp.dot(scaled, gu[which, span, :], preferred_element_type=f32)
            if index == 0:
                act[which] = term
            else:
                act[which] += term
    factor = lax.rsqrt(square / (count * width) + norm_eps)
    gate_out = act[0] * factor
    inner = (gate_out * sigmoid(gate_out) * (act[1] * factor)).astype(bf16)

    load_down.wait()
    for index in reversed(range(count)):
        target = peer(index)
        span = pl.ds(pl.multiple_of(target * width, width), width)
        term = jnp.dot(inner, down[:, span], preferred_element_type=f32).astype(bf16)
        if index == 0:
            feed = term.astype(f32)
        else:
            feed_send[index] = term
            copy = remote(
                feed_send.at[index], feed_recv.at[me], feed_sems.at[0, index], feed_sems.at[1, me], target
            )
            copy.start()
            sends.append(copy)
    for index in range(1, count):
        src = peer(index)
        remote(
            feed_send.at[index], feed_recv.at[src], feed_sems.at[0, index], feed_sems.at[1, src], src
        ).wait_recv()
        feed += feed_recv[src].astype(f32)
    final = (mid_all[me].astype(f32) + feed).astype(bf16)
    for s in range(steps):
        hidden_out[s] = final[cut[s]]
    store_hidden = pltpu.make_async_copy(hidden_out, out_hidden, local_sem.at[len(loads) + 2])
    store_hidden.start()
    half_copy.wait_send()
    for copy in sends:
        copy.wait_send()
    store_conv.wait()
    store_state.wait()
    store_hidden.wait()


def finish_kernel(*refs):
    sources, targets, held, sems = refs[:3], refs[3:6], refs[6:9], refs[9]
    inward, outward = [], []
    for source, target, buffer in zip(sources, targets, held):
        cuts = 4 if source.shape[0] % 4 == 0 else 1
        size = source.shape[0] // cuts
        for cut in range(cuts):
            span, place = pl.ds(cut * size, size), len(inward)
            inward.append(
                pltpu.make_async_copy(source.at[span], buffer.at[span], sems.at[0, place])
            )
            outward.append(
                pltpu.make_async_copy(buffer.at[span], target.at[span], sems.at[1, place])
            )
    for copy in inward:
        copy.start()
    for first, second in zip(inward, outward):
        first.wait()
        second.start()
    for copy in outward:
        copy.wait()


def in_one_kernel(
    hidden,
    attn_gain,
    w_qkvz,
    w_ab,
    conv_weight,
    decay_log,
    dt_bias,
    norm_gain,
    w_out,
    ffn_gain,
    w_gu,
    w_down,
    state,
    conv_state,
):
    count = lax.axis_size("tensor")
    steps, seqs, width = hidden.shape
    rows, full, units = steps * seqs, count * width, w_down.shape[0]
    kept = conv_state.shape[1]
    planes = (lax.axis_size("groups"), lax.axis_size("dp"))
    plane_count = planes[0] * planes[1]
    f32, bf16 = jnp.float32, jnp.bfloat16
    anywhere = pl.BlockSpec(memory_space=pl.ANY)
    scalar = pl.BlockSpec(memory_space=pltpu.SMEM)
    in_hbm = pl.BlockSpec(memory_space=pltpu.HBM)
    in_specs = [in_hbm] * 5 + [scalar] * 2 + [in_hbm] * 7
    vmem = pltpu.VMEM
    pair = pltpu.SemaphoreType.DMA((2, count))
    out = pl.pallas_call(
        functools.partial(mixer_kernel, count, planes),
        out_shape=(
            jax.ShapeDtypeStruct(hidden.shape, bf16),
            jax.ShapeDtypeStruct((seqs, HEAD, HEAD), f32),
            jax.ShapeDtypeStruct((kept, seqs, 2 * HEAD), bf16),
        ),
        in_specs=in_specs,
        out_specs=(anywhere,) * 3,
        scratch_shapes=[
            vmem((count, rows, width), bf16),
            vmem((full, 3 * HEAD), bf16),
            vmem((2, full), bf16),
            vmem((kept + 1, 2 * HEAD), bf16),
            vmem((HEAD, width), bf16),
            vmem((2, full, units), bf16),
            vmem((units, full), bf16),
            vmem((seqs, HEAD, HEAD), f32),
            vmem((kept, seqs, 2 * HEAD), bf16),
            vmem((2, full // 128, 128), bf16),
            vmem((1, HEAD), bf16),
            vmem((2, count, 1, width), f32),
            vmem((seqs, 2 * HEAD, HEAD), bf16),
            vmem((seqs, 8, HEAD), f32),
            vmem((seqs, 8, HEAD), f32),
            vmem((seqs, HEAD), f32),
            vmem((rows, HEAD), bf16),
            vmem((rows, HEAD), bf16),
            vmem((count, rows, HEAD), bf16),
            vmem((plane_count, count - 1, HEAD // plane_count, width), bf16),
            vmem((count, rows, width), bf16),
            vmem((count, rows, width), bf16),
            vmem((count, rows, width), bf16),
            vmem((2, rows, units), f32),
            vmem(hidden.shape, bf16),
            vmem((kept, seqs, 2 * HEAD), bf16),
            pltpu.SemaphoreType.DMA((20,)),
            pair,
            pltpu.SemaphoreType.DMA((2,)),
            pair,
            pair,
            pltpu.SemaphoreType.DMA((2, plane_count)),
            pair,
            pair,
        ],
        compiler_params=pltpu.CompilerParams(
            collective_id=0, has_side_effects=True, vmem_limit_bytes=63 * 2**20
        ),
    )(
        hidden,
        attn_gain.reshape(full // 128, 128),
        w_qkvz.reshape(full, 3 * HEAD),
        w_ab.reshape(full, 2).T,
        conv_weight.reshape(kept + 1, 2 * HEAD),
        decay_log,
        dt_bias,
        norm_gain.reshape(1, HEAD),
        w_out,
        ffn_gain.reshape(full // 128, 128),
        w_gu,
        w_down,
        state.reshape(seqs, HEAD, HEAD),
        conv_state.reshape(seqs, kept, 2 * HEAD).transpose(1, 0, 2),
    )
    next_hidden, next_state, next_conv = pl.pallas_call(
        finish_kernel,
        out_shape=tuple(jax.ShapeDtypeStruct(a.shape, a.dtype) for a in out),
        in_specs=[anywhere] * 3,
        out_specs=(anywhere,) * 3,
        scratch_shapes=[pltpu.VMEM(a.shape, a.dtype) for a in out]
        + [pltpu.SemaphoreType.DMA((2, 12))],
        compiler_params=pltpu.CompilerParams(vmem_limit_bytes=63 * 2**20),
    )(*out)
    return (
        next_hidden,
        next_state[:, None],
        next_conv.transpose(1, 0, 2)[:, :, None],
    )


def solution(mesh):
    placed = (
        P(None, ("groups", "dp"), "tensor"),
        P(),
        P(None, "tensor", None),
        P(None, "tensor", None),
        P(None, "tensor", None),
        P("tensor"),
        P("tensor"),
        P(),
        P("tensor", None),
        P(),
        P(None, None, "tensor"),
        P("tensor", None),
        P(("groups", "dp"), "tensor", None, None),
        P(("groups", "dp"), None, "tensor", None),
    )
    out_placed = (placed[0], placed[12], placed[13])

    def whole(*args):
        fits = lane_tiles_fit(mesh, args[0].shape[2], args[11].shape[0])
        one_head = args[2].shape[1] == mesh.shape["tensor"]
        body = in_one_kernel if fits and one_head else on_device
        return jax.shard_map(
            body, mesh=mesh, in_specs=placed, out_specs=out_placed, check_vma=False
        )(*args)

    return whole
```
